32 devices in a mesh: grp: 4 (over y, x), cand: 8 (over z, core).
Axes of the slice: x: 2, y: 2, z: 4, core: 2. Of those that a mesh axis runs over, the one named last changes fastest.
Arguments:
- node_emb: bfloat16 [8, 512, 512], P('cand'), may hold values from -6 to 6
- rel_emb: float32 [900, 512], P('grp'), may hold values from -6 to 6
- w_in: bfloat16 [512, 512], replicated, may hold values from -0.25 to 0.25
- w_self: bfloat16 [512, 512], replicated, may hold values from -1 to 1
- rel_score: float32 [900, 512], replicated, may hold values from -7 to 7
- mirror_blocks: int32 [4, 8, 8, 1], P('grp', 'cand'), may hold values from 0 to 3
- adj_values: bfloat16 [4, 8, 192, 128, 128], P('grp', 'cand'), may hold values from -0.0390625 to 0.0390625
- adj_source: int32 [4, 8, 192], P('grp', 'cand'), may hold values from 0 to 7
- adj_target: int32 [4, 8, 192], P('grp', 'cand'), may hold values from 0 to 3
- adj_relation: int32 [4, 8, 192], P('grp', 'cand'), may hold values from 0 to 224
- live_blocks: int32 [4, 8], P('grp', 'cand'), may hold values from 48 to 192, as said below
- query_head: int32 [1024], replicated, may hold values from 0 to 4095
- query_rel: int32 [1024], replicated, may hold values from 0 to 899
- allowed: int32 [1024, 8], replicated, may hold values from 0 to 31, as said below
- true_tail: int32 [1024], replicated, may hold values from 0 to 4095, as said below
Outputs:
- h_out: bfloat16 [8, 512, 512], P('cand', 'grp')
- loss: float32 [1024], replicated
- grad_h: float32 [8, 512, 512], P('cand', 'grp')
- grad_rel: float32 [900, 512], P('grp')
- grad_w_in: float32 [512, 512], replicated
- grad_w_self: float32 [512, 512], replicated
The draws below stay inside these ranges and needn't reach their ends.
Inputs may be any that keep to these rules, and one draw needn't show every extreme that they name: `live_blocks`: blocks from this count on are padding; on some device all 192 blocks are live. `allowed`: ids of blocks of 128 concepts; a query may name a block twice. `true_tail`: lies in one of the query's allowed blocks.
All inputs are finite; a program needn't handle non-finite values.
Results may differ from the reference program's by a relative error of at most 0.011.
Values may be sent and summed in bfloat16 or wider, within the bound.
No kernel may reach another device: no remote copies, remote signals or barrier semaphores. Data moves between devices by JAX's collectives and lax.ppermute only.
A program may use at most 128 MiB of HBM per device.

```python
import math
import jax
import jax.numpy as jnp
import numpy as np
from jax import lax

D = 512
REL = 900
BLOCK = 128
SLOT = 1
K_ALLOW = 8
NODE_DEV = 512
ADJ_BLK = 192
QUERIES = 1024
NODES = 4096
N_GRP = 4
N_CAND = 8


def sign_pattern(key):
    return jnp.where(jax.random.uniform(jax.random.fold_in(key, 77), (D,), jnp.float32) < 0.5, -1.0, 1.0)


def draw_w_self(key, part):
    rough = jnp.clip(jax.random.normal(jax.random.fold_in(key, 31), (D, D), jnp.float32), -4.0, 4.0) * D ** (-0.5)
    along = jnp.clip(jax.random.normal(jax.random.fold_in(key, 32), (D,), jnp.float32), -3.0, 3.0) * D ** (-0.5)
    value = rough + 2.0 * along[:, None] * sign_pattern(key)[None, :]
    return jnp.clip(value, -1.0, 1.0).astype(jnp.bfloat16)


def draw_rel_score(key, part):
    signs = jnp.where(jax.random.uniform(jax.random.fold_in(key, 1), (REL, D), jnp.float32) < 0.5, -1.0, 1.0)
    level = jnp.exp(jax.random.uniform(jax.random.fold_in(key, 4), (REL, 1), jnp.float32, jnp.log(5.5), jnp.log(7.5)))
    rough = jax.random.uniform(jax.random.fold_in(key, 5), (REL, D), jnp.float32, 0.9, 1.05)
    drawn = jnp.clip(signs * level * rough, -7.0, 7.0)
    order = jax.random.permutation(jax.random.fold_in(key, 6), REL)
    aligned = (order < max(1, REL // 4))[:, None]
    row_sign = jnp.where(jax.random.uniform(jax.random.fold_in(key, 7), (REL, 1), jnp.float32) < 0.5, -1.0, 1.0)
    strength = jax.random.uniform(jax.random.fold_in(key, 8), (REL, 1), jnp.float32, 6.6, 7.0)
    wobble = jax.random.uniform(jax.random.fold_in(key, 9), (REL, D), jnp.float32, 0.97, 1.0)
    lined = jnp.clip(row_sign * strength * wobble * sign_pattern(key)[None, :], -7.0, 7.0)
    return jnp.where(aligned, lined, drawn)


def draw_live_blocks(key, part):
    counts = jax.random.randint(key, (N_GRP * N_CAND,), ADJ_BLK // 4, ADJ_BLK + 1)
    busiest = jax.random.randint(jax.random.fold_in(key, 3), (), 0, N_GRP * N_CAND)
    counts = jnp.where(jnp.arange(N_GRP * N_CAND) == busiest, ADJ_BLK, counts)
    return counts.reshape(N_GRP, N_CAND).astype(jnp.int32)


def draw_query_head(key, part):
    base_key = jax.random.fold_in(key, 21)
    share = NODE_DEV // N_GRP
    share_count = N_GRP * N_CAND
    cover = jax.random.permutation(jax.random.fold_in(base_key, 1), share_count)
    extra = jax.random.randint(jax.random.fold_in(base_key, 2), (QUERIES,), 0, share_count)
    picks = jnp.where(jnp.arange(QUERIES) < share_count, jnp.pad(cover, (0, QUERIES - share_count)), extra)
    picks = jax.random.permutation(jax.random.fold_in(base_key, 3), picks)
    offset = jax.random.randint(jax.random.fold_in(base_key, 4), (QUERIES,), 0, share)
    offset = jnp.where(picks == 0, 0, jnp.where(picks == share_count - 1, share - 1, offset))
    return (picks * share + offset).astype(jnp.int32)


def allowed_helper(key):
    base_key = jax.random.fold_in(key, 11)
    block_count = NODES // BLOCK
    blocks = jax.random.randint(base_key, (QUERIES, K_ALLOW), 0, block_count)
    column = jax.random.randint(jax.random.fold_in(base_key, 1), (QUERIES,), 0, K_ALLOW)
    cover = jax.random.permutation(jax.random.fold_in(base_key, 3), block_count)
    order = jax.random.permutation(jax.random.fold_in(base_key, 4), QUERIES)
    current = jnp.take_along_axis(blocks, column[:, None], axis=1)[:, 0]
    padded_cover = jnp.pad(cover, (0, QUERIES - block_count))
    chosen = jnp.where(order < block_count, jnp.take(padded_cover, order), current)
    blocks = jnp.where(jnp.arange(K_ALLOW)[None, :] == column[:, None], chosen[:, None], blocks)
    offset = jax.random.randint(jax.random.fold_in(base_key, 2), (QUERIES,), 0, BLOCK)
    offset = jnp.where(chosen == 0, 0, jnp.where(chosen == block_count - 1, BLOCK - 1, offset))
    return (blocks.astype(jnp.int32), (chosen * BLOCK + offset).astype(jnp.int32))


def draw_allowed(key, part):
    blocks, tails = allowed_helper(key)
    return blocks


def draw_true_tail(key, part):
    blocks, tails = allowed_helper(key)
    return tails


def plant(values, stream_key, low, high):
    longest = values.shape.index(max(values.shape))
    spots = []
    for shift in (0, 1):
        where = [jax.random.randint(jax.random.fold_in(stream_key, axis), (), 0, length) for axis, length in enumerate(values.shape)]
        where[longest] = (where[longest] + shift) % values.shape[longest]
        spots.append(tuple(where))
    return values.at[spots[0]].set(low).at[spots[1]].set(high)


def levels(own_key, extent, pieces, least, top_value):
    loudness, own = 1.0, jax.random.fold_in(own_key, 6)
    for axis_at, blocks in pieces:
        heights = jnp.exp(jax.random.uniform(jax.random.fold_in(own, axis_at), (blocks,), jnp.float32, least / len(pieces), top_value / len(pieces)))
        loudness = loudness * jnp.repeat(heights, extent[axis_at] // blocks).reshape([-1 if axis == axis_at else 1 for axis in range(len(extent))])
    return loudness


def rank_bounds(number_of, lean):
    portions = [(1 << 20) // math.isqrt(grade ** lean) + 1 for grade in range(1, number_of + 1)]
    deviation = 1 + sum(portions) // (1 << 30)
    return np.cumsum(np.array([max(1, weight // deviation) for weight in portions]))


def ranked(own_key, shape, count, skew):
    table = rank_bounds(count, skew)
    lot = jax.random.randint(jax.random.fold_in(own_key, 1), shape, 0, int(table[count - 1]))
    grade = jnp.searchsorted(jnp.asarray(table, jnp.int32), lot, side="right")
    return jax.random.permutation(jax.random.fold_in(own_key, 2), count)[grade].astype(jnp.int32)


def gaussian(stream_key, dims, deviation, reach, cuts=(), kind=jnp.bfloat16):
    gain = levels(stream_key, dims, cuts, -0.22, 0.18) if cuts else 1.0
    result = jax.random.normal(stream_key, dims, jnp.float32) * deviation * gain
    return jnp.minimum(jnp.maximum(result, -reach), reach).astype(kind)


def setup_inputs(seed: int = 0) -> dict:
    keys = jax.random.split(jax.random.key(seed), 16)
    node_emb = gaussian(keys[0], (N_CAND, NODE_DEV, D), 1.0, 6.0, ((0, 8),))
    rel_emb = gaussian(keys[1], (REL, D), 1.0, 6.0, ((0, 4),), jnp.float32)
    w_in = gaussian(keys[2], (D, D), D ** -0.5, 0.25)
    w_self = draw_w_self(jax.random.fold_in(keys[15], 71), 0)
    rel_score = draw_rel_score(jax.random.fold_in(keys[15], 71), 0)
    mirror_blocks = plant(jax.random.randint(keys[5], (N_GRP, N_CAND, N_CAND, SLOT), 0, NODE_DEV // BLOCK), jax.random.fold_in(keys[5], 1), 0, (NODE_DEV // BLOCK) - 1).astype(jnp.int32)
    adj_values = gaussian(keys[6], (N_GRP, N_CAND, ADJ_BLK, BLOCK, BLOCK), (ADJ_BLK * N_GRP * BLOCK * BLOCK // NODE_DEV) ** -0.5, 0.0390625, ((0, 4), (1, 8)))
    adj_source = plant(jax.random.randint(keys[7], (N_GRP, N_CAND, ADJ_BLK), 0, N_CAND * SLOT), jax.random.fold_in(keys[7], 1), 0, (N_CAND * SLOT) - 1).astype(jnp.int32)
    adj_target = plant(jax.random.randint(keys[8], (N_GRP, N_CAND, ADJ_BLK), 0, NODE_DEV // BLOCK), jax.random.fold_in(keys[8], 1), 0, (NODE_DEV // BLOCK) - 1).astype(jnp.int32)
    adj_relation = plant(ranked(keys[9], (N_GRP, N_CAND, ADJ_BLK), REL // N_GRP, 2), jax.random.fold_in(keys[9], 3), 0, (REL // N_GRP) - 1).astype(jnp.int32)
    live_blocks = draw_live_blocks(jax.random.fold_in(keys[15], 71), 0)
    query_head = draw_query_head(jax.random.fold_in(keys[15], 71), 0)
    query_rel = plant(ranked(keys[12], (QUERIES,), REL, 2), jax.random.fold_in(keys[12], 3), 0, REL - 1).astype(jnp.int32)
    allowed = draw_allowed(jax.random.fold_in(keys[15], 71), 0)
    true_tail = draw_true_tail(jax.random.fold_in(keys[15], 71), 0)
    return dict(node_emb=node_emb, rel_emb=rel_emb, w_in=w_in, w_self=w_self, rel_score=rel_score, mirror_blocks=mirror_blocks, adj_values=adj_values, adj_source=adj_source, adj_target=adj_target, adj_relation=adj_relation, live_blocks=live_blocks, query_head=query_head, query_rel=query_rel, allowed=allowed, true_tail=true_tail)


NEG_FILL = -1.0e30
HIGH = lax.Precision.HIGHEST


def reference(node_emb, rel_emb, w_in, w_self, rel_score, mirror_blocks, adj_values, adj_source, adj_target, adj_relation, live_blocks, query_head, query_rel, allowed, true_tail):
    tile_count = NODE_DEV // BLOCK
    rels_local = REL // N_GRP
    node_total = N_CAND * NODE_DEV
    nodes = node_emb.reshape(node_total, D)
    tiled_nodes = nodes.reshape(N_CAND * tile_count, BLOCK, D)
    grp_ids = jnp.arange(N_GRP, dtype=jnp.int32)[:, None, None]
    cand_ids = jnp.arange(N_CAND, dtype=jnp.int32)[None, :, None]
    owner = adj_source // SLOT
    mirror_flat = mirror_blocks.reshape(N_GRP, N_CAND, N_CAND * SLOT)
    local_source = jnp.take_along_axis(mirror_flat, adj_source, axis=2)
    block_total = N_GRP * N_CAND * ADJ_BLK
    stride = math.gcd(block_total, 64)
    turns = block_total // stride
    source_tile = (owner * tile_count + local_source).reshape(turns, stride).astype(jnp.int32)
    target_tile = (cand_ids * tile_count + adj_target).reshape(turns, stride).astype(jnp.int32)
    relation_ids = (grp_ids * rels_local + adj_relation).reshape(turns, stride).astype(jnp.int32)
    live_mask = (jnp.arange(ADJ_BLK, dtype=jnp.int32)[None, None, :] < live_blocks[:, :, None]).astype(jnp.float32).reshape(turns, stride)
    tile_values = adj_values.reshape(turns, stride, BLOCK, BLOCK)
    packed = (tile_values, source_tile, target_tile, relation_ids, live_mask)

    def forward_turn(partial_value, inputs_now):
        values_now, source_now, target_now, relation_now, live_now = inputs_now
        composed = (tiled_nodes[source_now].astype(jnp.float32) - rel_emb[relation_now][:, None, :]).astype(jnp.bfloat16)
        messages = jnp.einsum("bij,bjd->bid", values_now.astype(jnp.float32), composed.astype(jnp.float32), precision=HIGH)
        messages = messages * live_now[:, None, None]
        return partial_value.at[target_now].add(messages), None

    partial_value, ignored = lax.scan(forward_turn, jnp.zeros((N_CAND * tile_count, BLOCK, D), jnp.float32), packed)
    aggregate = partial_value.reshape(node_total, D).astype(jnp.bfloat16)
    pre_act = jnp.dot(aggregate, w_in, preferred_element_type=jnp.float32) + jnp.dot(nodes, w_self, preferred_element_type=jnp.float32)
    activated = jnp.tanh(pre_act)
    h_out = activated.astype(jnp.bfloat16)

    cand_rows = h_out.astype(jnp.float32)
    queries = cand_rows[query_head] + rel_score[query_rel]
    scale = D ** -0.5
    cross = jnp.dot(queries, cand_rows.T, precision=HIGH)
    scores = -scale * (jnp.sum(queries * queries, axis=1)[:, None] + jnp.sum(cand_rows * cand_rows, axis=1)[None, :] - 2.0 * cross)
    block_total_c = node_total // BLOCK
    block_ok = jnp.any(allowed[:, :, None] == jnp.arange(block_total_c, dtype=jnp.int32)[None, None, :], axis=1)
    allowed_mask = jnp.repeat(block_ok, BLOCK, axis=1)
    tail_pick = true_tail[:, None] == jnp.arange(node_total, dtype=jnp.int32)[None, :]
    row_max = jnp.max(jnp.where(allowed_mask, scores, NEG_FILL), axis=1)
    row_total = jnp.sum(jnp.exp(jnp.where(allowed_mask, scores - row_max[:, None], NEG_FILL)), axis=1)
    truth = jnp.sum(jnp.where(tail_pick, scores, 0.0), axis=1)
    log_norm = row_max + jnp.log(row_total)
    loss = log_norm - truth

    prob = jnp.exp(jnp.where(allowed_mask, scores - log_norm[:, None], NEG_FILL))
    grad_score = (prob - tail_pick.astype(jnp.float32)) / QUERIES
    query_grad = 2.0 * scale * (jnp.dot(grad_score, cand_rows, precision=HIGH) - queries * jnp.sum(grad_score, axis=1)[:, None])
    cand_grad = 2.0 * scale * (jnp.dot(grad_score.T, queries, precision=HIGH) - cand_rows * jnp.sum(grad_score, axis=0)[:, None])
    row_grad = cand_grad + jnp.zeros((node_total, D), jnp.float32).at[query_head].add(query_grad)
    pre_grad = (row_grad * (1.0 - activated * activated)).astype(jnp.bfloat16)
    grad_w_in = jnp.dot(aggregate.T, pre_grad, preferred_element_type=jnp.float32)
    grad_w_self = jnp.dot(nodes.T, pre_grad, preferred_element_type=jnp.float32)
    agg_grad = jnp.dot(pre_grad, w_in.T, preferred_element_type=jnp.float32).astype(jnp.bfloat16)
    agg_tiles = agg_grad.reshape(N_CAND * tile_count, BLOCK, D)

    def backward_turn(carry, inputs_now):
        node_acc, relation_acc = carry
        values_now, source_now, target_now, relation_now, live_now = inputs_now
        composed_grad = jnp.einsum("bij,bid->bjd", values_now.astype(jnp.float32), agg_tiles[target_now].astype(jnp.float32), precision=HIGH)
        composed_grad = composed_grad * live_now[:, None, None]
        node_acc = node_acc.at[source_now].add(composed_grad)
        relation_acc = relation_acc.at[relation_now].add(-jnp.sum(composed_grad, axis=1))
        return (node_acc, relation_acc), None

    start = (jnp.zeros((N_CAND * tile_count, BLOCK, D), jnp.float32), jnp.zeros((REL, D), jnp.float32))
    (node_acc, grad_rel), ignored = lax.scan(backward_turn, start, packed)
    grad_h = node_acc.reshape(node_total, D) + jnp.dot(pre_grad, w_self.T, preferred_element_type=jnp.float32)
    return (h_out.reshape(N_CAND, NODE_DEV, D), loss, grad_h.reshape(N_CAND, NODE_DEV, D), grad_rel, grad_w_in, grad_w_self)
```

```python
import functools

import jax
import jax.numpy as jnp
from jax import lax
from jax.experimental import pallas as pl
from jax.experimental.pallas import tpu as pltpu
from jax.sharding import PartitionSpec as P

NEG_FILL = -1e30
BF = jnp.bfloat16
F32 = jnp.float32
NT = (((1,), (1,)), ((), ()))
TN = (((0,), (0,)), ((), ()))
VMEM_BYTES = 60 * 1024 * 1024


def dot(a, b):
    return jnp.dot(a, b, preferred_element_type=F32)


def dot_nt(a, b, precision=None):
    return lax.dot_general(a, b, NT, precision=precision, preferred_element_type=F32)


def split(x):
    hi = x.astype(BF)
    return hi, (x - hi.astype(F32)).astype(BF)


def params(**kw):
    return pltpu.CompilerParams(vmem_limit_bytes=VMEM_BYTES, **kw)


def fixed(shape):
    return pl.BlockSpec(shape, lambda *a: (0,) * len(shape), pipeline_mode=pl.Buffered(1))


def fold_kernel(
    tiles, per, src, tgt, rel, live, a_ref, anh_ref, anl_ref, at_ref, w_ref, wth_ref, wtl_ref, acc, wacc
):
    step = pl.program_id(0)
    slots, block, rows = at_ref.shape

    @pl.when(step == 0)
    def _():
        acc[...] = jnp.zeros_like(acc)
        wacc[...] = jnp.zeros_like(wacc)

    ones = jnp.ones((8, block), BF)
    sums = dot_nt(ones, a_ref[...].reshape(per * block, block))
    for i in range(per):
        b = step * per + i

        @pl.when(b < live[0])
        def _():
            at = tgt[b] * slots + src[b]
            acc[at] = acc[at] + a_ref[i].astype(F32)
            row = pl.ds(rel[b], 1)
            wacc[tgt[b], row, :] = wacc[tgt[b], row, :] + sums[0:1, i * block : (i + 1) * block]

    @pl.when(step == pl.num_programs(0) - 1)
    def _():
        for t in range(tiles):
            at = slice(t * block, (t + 1) * block)
            for s in range(slots):
                part = acc[t * slots + s]
                hi, lo = split(part)
                anh_ref[at, s * block : (s + 1) * block] = hi
                anl_ref[at, s * block : (s + 1) * block] = lo
                at_ref[s, :, at] = part.T.astype(BF)
            w_ref[:, at] = wacc[t].astype(BF)
            hi, lo = split(wacc[t].T)
            wth_ref[at, :] = hi
            wtl_ref[at, :] = lo


def fold(adj, src, tgt, rel, live, slots, tiles, rel_rows):
    count, block, _ = adj.shape
    per = next(p for p in (16, 8, 4, 2, 1) if count % p == 0)
    rows = tiles * block
    shapes = [
        ((rows, slots * block), BF),
        ((rows, slots * block), BF),
        ((slots, block, rows), BF),
        ((rel_rows, rows), BF),
        ((rows, rel_rows), BF),
        ((rows, rel_rows), BF),
    ]
    return pl.pallas_call(
        functools.partial(fold_kernel, tiles, per),
        grid_spec=pltpu.PrefetchScalarGridSpec(
            num_scalar_prefetch=4,
            grid=(count // per,),
            in_specs=[pl.BlockSpec((per, block, block), lambda i, *a: (i, 0, 0))],
            out_specs=[fixed(s) for s, _ in shapes],
            scratch_shapes=[
                pltpu.VMEM((tiles * slots, block, block), F32),
                pltpu.VMEM((tiles, rel_rows, block), F32),
            ],
        ),
        out_shape=[jax.ShapeDtypeStruct(s, d) for s, d in shapes],
        compiler_params=params(),
        name="fold_adjacency",
    )(src, tgt, rel, live, adj)


def forward_kernel(slots, ids, *refs):
    anh_ref, anl_ref, wth_ref, wtl_ref, rel_ref, out_ref, outb_ref = refs[slots:]
    mirrors = jnp.concatenate([ref[0] for ref in refs[:slots]], axis=0)
    hi, lo = split(rel_ref[...])
    total = dot(anh_ref[...], mirrors) + dot(anl_ref[...], mirrors)
    total = total - (dot(wth_ref[...], hi) + dot(wth_ref[...], lo) + dot(wtl_ref[...], hi))
    out_ref[...] = total
    outb_ref[...] = total.astype(BF)


def forward(ids, nodes, anh, anl, wth, wtl, rel):
    slots = ids.shape[0]
    rows = anh.shape[0]
    _, block, width = nodes.shape
    rest = (anh, anl, wth, wtl, rel)
    return pl.pallas_call(
        functools.partial(forward_kernel, slots),
        grid_spec=pltpu.PrefetchScalarGridSpec(
            num_scalar_prefetch=1,
            grid=(1,),
            in_specs=[
                pl.BlockSpec((1, block, width), lambda i, ids, s=s: (ids[s], 0, 0))
                for s in range(slots)
            ]
            + [fixed(x.shape) for x in rest],
            out_specs=[fixed((rows, width)), fixed((rows, width))],
        ),
        out_shape=[
            jax.ShapeDtypeStruct((rows, width), F32),
            jax.ShapeDtypeStruct((rows, width), BF),
        ],
        compiler_params=params(),
        name="forward_partial",
    )(ids, *[nodes] * slots, *rest)


def activate_kernel(agg_ref, node_ref, win_ref, wself_ref, h_ref, *more):
    act = jnp.tanh(dot(agg_ref[...], win_ref[...]) + dot(node_ref[...], wself_ref[...]))
    h = act.astype(BF)
    h_ref[...] = h
    if more:
        d_ref, ht_ref = more
        d_ref[...] = (1.0 - act * act).astype(BF)
        ht_ref[...] = h.astype(F32).T.astype(BF)


def activate(agg, nodes, w_in, w_self, rows, flipped):
    total, width = agg.shape
    tall = pl.BlockSpec((rows, width), lambda i: (i, 0))
    return pl.pallas_call(
        activate_kernel,
        grid=(total // rows,),
        in_specs=[tall, tall, fixed(w_in.shape), fixed(w_self.shape)],
        out_specs=[tall] + [tall] * flipped + [pl.BlockSpec((width, rows), lambda i: (0, i))] * flipped,
        out_shape=[jax.ShapeDtypeStruct((total, width), BF)] * (1 + flipped)
        + [jax.ShapeDtypeStruct((width, total), BF)] * flipped,
        compiler_params=params(),
        name="activate",
    )(agg, nodes, w_in, w_self)


def score_kernel(block, total_q, flipped, h_ref, *refs):
    ht_ref = refs[0] if flipped else None
    q_ref, meta_ref, gs_ref, qg_ref, qb_ref, loss_ref, s_ref, hsq_ref = refs[flipped:]
    total, width = h_ref.shape
    qt = q_ref.shape[0]
    blocks = total // block
    scale = width ** (-0.5)

    def rows_of(b):
        return pl.ds(pl.multiple_of(b * block, block), block)

    @pl.when(pl.program_id(0) == 0)
    def _():
        def square(b, carry):
            x = h_ref[rows_of(b), :].astype(F32)
            norm = scale * jnp.sum(x * x, axis=1, keepdims=True)
            hsq_ref[rows_of(b), :] = jnp.broadcast_to(norm, (block, 128))
            return carry

        lax.fori_loop(0, blocks, square, 0)

    q = q_ref[...]
    qb_ref[...] = q.astype(BF)
    hi, lo = split(q * (2.0 * scale))
    qsq = scale * dot_nt(jnp.ones((8, width), F32), q * q, precision=lax.Precision.HIGHEST)[0:1]
    allowed = meta_ref[:-8, :]
    tail = meta_ref[meta_ref.shape[0] - 8 : meta_ref.shape[0] - 7, :]

    def first(b, top):
        hb = h_ref[rows_of(b), :]
        cross = dot_nt(hb, hi) + dot_nt(hb, lo)
        ok = jnp.max((allowed == b).astype(jnp.int32), axis=0, keepdims=True) > 0
        bias = jnp.where(ok, 0.0, NEG_FILL) - qsq
        hsq = jnp.concatenate([hsq_ref[rows_of(b), :]] * (qt // 128), axis=1)
        s = cross - hsq + bias
        s_ref[rows_of(b), :] = s
        return jnp.maximum(top, jnp.max(s.reshape(block // 8, 8, qt), axis=0))

    top = lax.fori_loop(0, blocks, first, jnp.full((8, qt), 2.0 * NEG_FILL, F32), unroll=4)
    top = jnp.max(top, axis=0, keepdims=True)
    row = lax.broadcasted_iota(jnp.int32, (block, qt), 0)

    def second(b, carry):
        norm, truth = carry
        s = s_ref[rows_of(b), :]
        e = jnp.exp(s - top)
        s_ref[rows_of(b), :] = e
        at_tail = jnp.where(row == tail - b * block, s, 0.0)
        norm = norm + jnp.sum(e.reshape(block // 8, 8, qt), axis=0)
        truth = truth + jnp.sum(at_tail.reshape(block // 8, 8, qt), axis=0)
        return norm, truth

    zero = jnp.zeros((8, qt), F32)
    norm, truth = lax.fori_loop(0, blocks, second, (zero, zero))
    norm = jnp.sum(norm, axis=0, keepdims=True)
    truth = jnp.sum(truth, axis=0, keepdims=True)
    loss_ref[...] = top + jnp.log(norm) - truth
    inverse = 1.0 / norm

    def third(b, carry):
        e = s_ref[rows_of(b), :]
        picked = jnp.where(row == tail - b * block, 1.0, 0.0)
        gs_ref[rows_of(b), :] = ((e * inverse - picked) * (1.0 / total_q)).astype(BF)
        return carry

    lax.fori_loop(0, blocks, third, 0)
    if flipped:
        pulled = dot(ht_ref[...], gs_ref[...]).T
    else:
        pulled = lax.dot_general(gs_ref[...], h_ref[...], TN, preferred_element_type=F32)
    rowsum = (norm * inverse - 1.0) * (1.0 / total_q)
    rowsum = jnp.broadcast_to(rowsum, (128, qt)).T[:, 0:1]
    qg_ref[...] = (2.0 * scale * (pulled - q * rowsum)).astype(BF)


def score(h, ht, q, meta, block, qt):
    flipped = len(ht)
    total, width = h.shape
    total_q = q.shape[0]
    return pl.pallas_call(
        functools.partial(score_kernel, block, total_q, flipped),
        grid=(total_q // qt,),
        in_specs=[
            fixed(h.shape),
            *[fixed(x.shape) for x in ht],
            pl.BlockSpec((qt, width), lambda i: (i, 0)),
            pl.BlockSpec((meta.shape[0], qt), lambda i: (0, i)),
        ],
        out_specs=[
            pl.BlockSpec((total, qt), lambda i: (0, i)),
            pl.BlockSpec((qt, width), lambda i: (i, 0)),
            pl.BlockSpec((qt, width), lambda i: (i, 0)),
            pl.BlockSpec((1, qt), lambda i: (0, i)),
        ],
        out_shape=[
            jax.ShapeDtypeStruct((total, total_q), BF),
            jax.ShapeDtypeStruct((total_q, width), BF),
            jax.ShapeDtypeStruct((total_q, width), BF),
            jax.ShapeDtypeStruct((1, total_q), F32),
        ],
        scratch_shapes=[pltpu.VMEM((total, qt), F32), pltpu.VMEM((total, 128), F32)],
        compiler_params=params(),
        name="score",
    )(h, *ht, q, meta)


def backward_kernel(
    tiles,
    slot_count,
    recompute,
    pos,
    gs_ref,
    qb_ref,
    qg_ref,
    head_ref,
    h_ref,
    d_ref,
    agg_ref,
    node_ref,
    win_ref,
    wself_ref,
    at_ref,
    w_ref,
    pre_ref,
    owned_ref,
    grel_ref,
    gwin_ref,
    gwself_ref,
):
    c = pl.program_id(0)
    count = pl.num_programs(0)
    rows, width = h_ref.shape
    total_q = qb_ref.shape[0]
    block = rows // tiles
    scale = width ** (-0.5)

    @pl.when(c == 0)
    def _():
        owned_ref[...] = jnp.zeros_like(owned_ref)
        grel_ref[...] = jnp.zeros_like(grel_ref)
        gwin_ref[...] = jnp.zeros_like(gwin_ref)
        gwself_ref[...] = jnp.zeros_like(gwself_ref)

    gs = gs_ref[...]
    colsum = dot(gs, jnp.ones((total_q, 128), BF))
    colsum = jnp.concatenate([colsum] * (width // 128), axis=1)
    row = lax.broadcasted_iota(jnp.int32, (rows, total_q), 0) + c * rows
    picked = jnp.where(row == head_ref[0:1, :], 1.0, 0.0).astype(BF)
    grad = 2.0 * scale * (dot(gs, qb_ref[...]) - h_ref[...].astype(F32) * colsum)
    grad = grad + dot(picked, qg_ref[...])
    if recompute:
        act = jnp.tanh(dot(agg_ref[...], win_ref[...]) + dot(node_ref[...], wself_ref[...]))
        slope = 1.0 - act * act
    else:
        slope = d_ref[...].astype(F32)
    pre = (grad * slope).astype(BF)

    @pl.when(c == pos[count])
    def _():
        pre_ref[...] = pre

    agg_grad = dot_nt(pre, win_ref[...]).astype(BF)
    for s in range(slot_count):
        back = dot(at_ref[0, s, 0:block, :], agg_grad)
        which = at_ref[0, s, block : block + 16, :].astype(F32)[0:1, :]
        for t in range(tiles):
            owned_ref[t] = owned_ref[t] + jnp.where(which == t, back, 0.0)
    grel_ref[...] = grel_ref[...] - dot(w_ref[0], agg_grad)
    gwin_ref[...] += lax.dot_general(agg_ref[...], pre, TN, preferred_element_type=F32)
    gwself_ref[...] += lax.dot_general(node_ref[...], pre, TN, preferred_element_type=F32)


def backward(pos, gs, qb, qg, head, h, d, agg, nodes, w_in, w_self, at, w, tiles, recompute):
    total, width = h.shape
    count, slot_count, at_rows, rows = at.shape
    rel_rows = w.shape[1]
    total_q = qb.shape[0]
    block = rows // tiles
    tall = pl.BlockSpec((rows, width), lambda i, pos: (i, 0))
    return pl.pallas_call(
        functools.partial(backward_kernel, tiles, slot_count, recompute),
        grid_spec=pltpu.PrefetchScalarGridSpec(
            num_scalar_prefetch=1,
            grid=(count,),
            in_specs=[
                pl.BlockSpec((rows, total_q), lambda i, pos: (i, 0)),
                fixed(qb.shape),
                fixed(qg.shape),
                fixed(head.shape),
                tall,
                tall,
                tall,
                tall,
                fixed(w_in.shape),
                fixed(w_self.shape),
                pl.BlockSpec((1, slot_count, at_rows, rows), lambda i, pos: (pos[i], 0, 0, 0)),
                pl.BlockSpec((1, rel_rows, rows), lambda i, pos: (i, 0, 0)),
            ],
            out_specs=[
                fixed((rows, width)),
                fixed((tiles, block, width)),
                fixed((rel_rows, width)),
                fixed((width, width)),
                fixed((width, width)),
            ],
        ),
        out_shape=[
            jax.ShapeDtypeStruct((rows, width), BF),
            jax.ShapeDtypeStruct((tiles, block, width), F32),
            jax.ShapeDtypeStruct((rel_rows, width), F32),
            jax.ShapeDtypeStruct((width, width), F32),
            jax.ShapeDtypeStruct((width, width), F32),
        ],
        compiler_params=params(),
        name="backward",
    )(pos, gs, qb, qg, head, h, d, agg, nodes, w_in, w_self, at, w)


def sum_over_grp(whole, whole_bf, grp_index, grp_count, share_rows):
    total = lax.dynamic_slice_in_dim(whole, grp_index * share_rows, share_rows, 0)
    for k in range(1, grp_count):
        part = lax.dynamic_slice_in_dim(whole_bf, (grp_index ^ k) * share_rows, share_rows, 0)
        got = lax.ppermute(part, "grp", [(i, i ^ k) for i in range(grp_count)])
        total = total + got.astype(F32)
    return total


def body(
    node_emb,
    rel_emb,
    w_in,
    w_self,
    rel_score,
    mirror_blocks,
    adj_values,
    adj_source,
    adj_target,
    adj_relation,
    live_blocks,
    query_head,
    query_rel,
    allowed,
    true_tail,
):
    cand_count = lax.axis_size("cand")
    grp_count = lax.axis_size("grp")
    grp_index = lax.axis_index("grp")
    cand_index = lax.axis_index("cand")
    nodes = node_emb[0]
    node_rows, width = nodes.shape
    block = adj_values.shape[-1]
    tiles = node_rows // block
    share_rows = node_rows // grp_count
    wanted = mirror_blocks[0, 0]
    slot_count = wanted.shape[1]
    slots = cand_count * slot_count
    total = cand_count * node_rows
    total_q = query_head.shape[0]
    rel_rows = -(-rel_emb.shape[0] // 128) * 128

    all_nodes = lax.all_gather(nodes, "cand", axis=0, tiled=True)
    anh, anl, at, w, wth, wtl = fold(
        adj_values[0, 0],
        adj_source[0, 0],
        adj_target[0, 0],
        adj_relation[0, 0],
        live_blocks[0],
        slots,
        tiles,
        rel_rows,
    )
    owners = jnp.arange(cand_count, dtype=jnp.int32)[:, None] * tiles
    rel_pad = jnp.pad(rel_emb, ((0, rel_rows - rel_emb.shape[0]), (0, 0)))
    partial, partial_bf = forward(
        (owners + wanted).reshape(-1),
        all_nodes.reshape(cand_count * tiles, block, width),
        anh,
        anl,
        wth,
        wtl,
        rel_pad,
    )
    own_agg = sum_over_grp(partial, partial_bf, grp_index, grp_count, share_rows).astype(BF)
    all_agg = lax.all_gather(own_agg, ("cand", "grp"), axis=0, tiled=True)
    rel_rows_q = jnp.take(rel_score, query_rel, axis=0)

    marks = jnp.broadcast_to(
        wanted.astype(BF).reshape(cand_count, slot_count, 1, 1),
        (cand_count, slot_count, 16, node_rows),
    )
    at = jnp.concatenate([at.reshape(cand_count, slot_count, block, node_rows), marks], axis=2)
    all_agg, at, w = lax.optimization_barrier((all_agg, at, w))
    pieces = [lax.dynamic_index_in_dim(at, cand_index, 0, keepdims=True)]
    for k in range(1, cand_count):
        piece = lax.dynamic_index_in_dim(at, (cand_index + k) % cand_count, 0, keepdims=True)
        shift = [(i, (i + k) % cand_count) for i in range(cand_count)]
        pieces.append(lax.ppermute(piece, "cand", shift))
    at_mine = jnp.concatenate(pieces, axis=0)
    pos = (cand_index - jnp.arange(cand_count, dtype=jnp.int32)) % cand_count
    pos = jnp.concatenate([pos, cand_index.astype(jnp.int32)[None]])
    w_all = lax.all_gather(w[None], "cand", axis=0, tiled=True)

    small = total <= 4096
    h, *more = activate(all_agg, all_nodes, w_in, w_self, node_rows, int(small))
    d, ht = (more[0], more[1:]) if small else (h, [])
    queries = jnp.take(h, query_head, axis=0).astype(F32) + rel_rows_q
    meta = jnp.concatenate(
        [
            allowed.T,
            jnp.broadcast_to(true_tail[None, :], (8, total_q)),
        ],
        axis=0,
    )
    qt = 256 if small else 128
    gs, qg, qb, loss = score(h, ht, queries, meta, block, qt)
    head = jnp.broadcast_to(query_head[None, :], (8, total_q))
    pre, owned, grel, gwin, gwself = backward(
        pos,
        gs,
        qb,
        qg,
        head,
        h,
        d,
        all_agg,
        all_nodes,
        w_in,
        w_self,
        at_mine,
        w_all,
        tiles,
        not small,
    )
    owned = owned.reshape(node_rows, width)
    node_grad = sum_over_grp(owned, owned.astype(BF), grp_index, grp_count, share_rows)
    first_row = cand_index * node_rows + grp_index * share_rows
    own_pre = lax.dynamic_slice_in_dim(pre, grp_index * share_rows, share_rows, 0)
    node_grad = node_grad + lax.dot_general(own_pre, w_self, NT, preferred_element_type=F32)
    h_own = lax.dynamic_slice_in_dim(h, first_row, share_rows, 0)
    return (
        h_own[None],
        loss[0],
        node_grad[None],
        grel[: rel_emb.shape[0]],
        gwin,
        gwself,
    )


def solution(mesh):
    return jax.shard_map(
        body,
        mesh=mesh,
        in_specs=(
            P("cand", None, None),
            P("grp", None),
            P(),
            P(),
            P(),
            P("grp", "cand", None, None),
            P("grp", "cand", None, None, None),
            P("grp", "cand", None),
            P("grp", "cand", None),
            P("grp", "cand", None),
            P("grp", "cand"),
            P(),
            P(),
            P(),
            P(),
        ),
        out_specs=(P("cand", "grp", None), P(), P("cand", "grp", None), P("grp", None), P(), P()),
        check_vma=False,
    )
```

```python
import functools

import jax
import jax.numpy as jnp
from jax import lax
from jax.experimental import pallas as pl
from jax.experimental.pallas import tpu as pltpu
from jax.sharding import PartitionSpec as P

NEG_FILL = -1e30
BF = jnp.bfloat16
F32 = jnp.float32
I32 = jnp.int32
MARK_ROWS = 16


def dot(a, b):
    return jnp.dot(a, b, preferred_element_type=F32)


def dot_nt(a, b):
    return lax.dot_general(a, b, (((1,), (1,)), ((), ())), preferred_element_type=F32)


def split(x):
    hi = x.astype(BF)
    return hi, (x - hi.astype(F32)).astype(BF)


def params(small, mebibytes):
    return pltpu.CompilerParams(vmem_limit_bytes=(mebibytes if small else 60) * 1024 * 1024)


def fixed(shape):
    return pl.BlockSpec(shape, lambda *a: (0,) * len(shape), pipeline_mode=pl.Buffered(1))


def shaped(*pairs):
    return [jax.ShapeDtypeStruct(s, d) for s, d in pairs]


def cost(micros):
    return pl.CostEstimate(flops=micros * 10**9, bytes_accessed=micros * 10**6, transcendentals=0)


def rows_at(index, size):
    return pl.ds(pl.multiple_of(index * size, size), size)


def fold_kernel(tiles, per, src, tgt, rel, live, want, core, a_ref, *refs):
    cat_ref, send_ref, acc, wacc, line, ids = refs
    step = pl.program_id(0)
    block = a_ref.shape[1]
    slots = want.shape[0]
    part_rows = block + MARK_ROWS
    rel_rows = (wacc.shape[0] - 8) // tiles
    count = line.shape[0]

    @pl.when(step == 0)
    def _():
        acc[...] = jnp.zeros_like(acc)
        wacc[...] = jnp.zeros_like(wacc)

    sums = dot_nt(jnp.ones((8, block), BF), a_ref[...].reshape(per * block, block))
    for i in range(per):
        b = step * per + i
        good = b < live[0]
        at = jnp.where(good, tgt[b] * slots + src[b], tiles * slots)
        acc[at] = acc[at] + a_ref[i].astype(F32)
        row = jnp.where(good, tgt[b] * rel_rows + rel[b], tiles * rel_rows)
        total = sums[0:1, i * block : (i + 1) * block]
        wacc[pl.ds(row, 1), :] = wacc[pl.ds(row, 1), :] + total
        line[pl.ds(b, 1), :] = jnp.where(good, total, 0.0)
        ids[pl.ds(b, 1), :] = jnp.zeros((1, block), F32) + (rel[b] * tiles + tgt[b]).astype(F32)

    @pl.when(step == pl.num_programs(0) - 1)
    def _():
        base = 2 * slots * block
        quarter = count // tiles
        for z in range(slots // 2):
            for t in range(tiles):
                at = slice(t * block, (t + 1) * block)
                those = slice(t * quarter, (t + 1) * quarter)
                tail = 2 * part_rows
                send_ref[z, tail : tail + quarter, at] = line[those, :].astype(BF)
                packed = ids[those, :].astype(I32)
                send_ref[z, tail + quarter : tail + 2 * quarter, at] = jnp.where(
                    lax.broadcasted_iota(I32, packed.shape, 1) < block // 2,
                    packed // tiles,
                    packed % tiles,
                ).astype(F32).astype(BF)
        for t in range(tiles):
            at = slice(t * block, (t + 1) * block)
            hi, lo = split(-wacc[t * rel_rows : (t + 1) * rel_rows, :].T)
            cat_ref[at, base : base + rel_rows] = hi
            cat_ref[at, base + rel_rows : base + 2 * rel_rows] = hi
            cat_ref[at, base + 2 * rel_rows :] = lo
            for s in range(slots):
                part = acc[t * slots + s]
                hi, lo = split(part)
                cat_ref[at, s * block : (s + 1) * block] = hi
                cat_ref[at, (slots + s) * block : (slots + s + 1) * block] = lo
                place = pl.multiple_of((s % 2 ^ core[0]) * part_rows, 16)
                send_ref[s // 2, pl.ds(place, block), at] = part.T.astype(BF)
                mark = jnp.zeros((MARK_ROWS, block), F32) + want[s].astype(F32)
                send_ref[s // 2, pl.ds(place + block, MARK_ROWS), at] = mark.astype(BF)


def fold(adj, src, tgt, rel, live, want, core, tiles, rel_rows):
    count, block, _ = adj.shape
    slots = want.shape[0]
    per = next(p for p in (48, 16, 8, 4, 2, 1) if count % p == 0)
    rows = tiles * block
    outs = [
        ((rows, 2 * slots * block + 3 * rel_rows), BF),
        ((slots // 2, 2 * (block + MARK_ROWS) + 2 * (count // tiles), rows), BF),
    ]
    return pl.pallas_call(
        functools.partial(fold_kernel, tiles, per),
        grid_spec=pltpu.PrefetchScalarGridSpec(
            num_scalar_prefetch=6,
            grid=(count // per,),
            in_specs=[pl.BlockSpec((per, block, block), lambda i, *a: (i, 0, 0))],
            out_specs=[fixed(s) for s, _ in outs],
            scratch_shapes=[
                pltpu.VMEM((tiles * slots + 1, block, block), F32),
                pltpu.VMEM((tiles * rel_rows + 8, block), F32),
                pltpu.VMEM((count, block), F32),
                pltpu.VMEM((count, block), F32),
            ],
        ),
        out_shape=shaped(*outs),
        compiler_params=params(slots <= 8, 60),
        cost_estimate=cost(8),
        name="fold_adjacency",
    )(src, tgt, rel, live, want, core, adj)


def stacked(shift, flip, cut, block):
    if shift == 0:
        return 0, None
    if flip < 3:
        return 1 + flip, (shift - 1) * block
    return (4, (shift - 1) * block) if shift < cut else (5, (shift - cut) * block)


def pick_kernel(planes, block, cut, plane, grp, mine, theirs, *refs):
    sources, (mine_ref, theirs_ref, sems) = refs[:-3], refs[-3:]
    flips = sources[0].shape[0] // block
    for wait in (False, True):
        for n, (ids, out_ref) in enumerate(((mine, mine_ref), (theirs, theirs_ref))):
            for s in range(planes):
                j = lax.rem(plane[0] - s + planes, planes)
                for a in range(1 if s == 0 or wait else flips):
                    which, row = stacked(s, a, cut, block)
                    if s == 0:
                        source = sources[0].at[rows_at(ids[j], block), :]
                    else:
                        source = sources[which].at[row : row + block, :]
                    target = out_ref.at[rows_at(j, block), :]
                    copy = pltpu.make_async_copy(source, target, sems.at[n, s])
                    if wait:
                        copy.wait()
                    elif s == 0:
                        copy.start()
                    else:

                        @pl.when((ids[j] ^ grp[0]) == a)
                        def _():
                            copy.start()


def pick(plane, grp, mine, theirs, sources, block):
    planes = mine.shape[0]
    out = ((planes * block, sources[0].shape[1]), BF)
    cut = 1 + sources[4].shape[0] // block
    anywhere = pl.BlockSpec(memory_space=pl.ANY)
    return pl.pallas_call(
        functools.partial(pick_kernel, planes, block, cut),
        grid_spec=pltpu.PrefetchScalarGridSpec(
            num_scalar_prefetch=4,
            grid=(1,),
            in_specs=[anywhere] * len(sources),
            out_specs=[fixed(out[0])] * 2,
            scratch_shapes=[pltpu.SemaphoreType.DMA((2, planes))],
        ),
        out_shape=shaped(out, out),
        compiler_params=params(planes <= 4, 6),
        name="pick_mirrors",
    )(plane, grp, mine, theirs, *sources)


def forward_kernel(block, rel_count, core, mine_ref, theirs_ref, cat_ref, rel_ref, out_ref, outb_ref, right):
    depth = 2 * mine_ref.shape[0]
    rel_rows = rel_ref.shape[0]
    inside = lax.broadcasted_iota(I32, rel_ref.shape, 0) < rel_count
    for j in range(mine_ref.shape[0] // block):
        at = slice(j * block, (j + 1) * block)
        for base in (0, depth // block):
            right[rows_at(base + 2 * j + core[0], block), :] = mine_ref[at, :]
            right[rows_at(base + 2 * j + 1 - core[0], block), :] = theirs_ref[at, :]
    hi, lo = split(jnp.where(inside, rel_ref[...], 0.0))
    for i, part in enumerate((hi, lo, hi)):
        right[2 * depth + i * rel_rows : 2 * depth + (i + 1) * rel_rows, :] = part
    total = dot(cat_ref[...], right[...])
    out_ref[...] = total
    outb_ref[...] = total.astype(BF)


def forward(core, mine, theirs, cat, rel, block):
    rows, depth = cat.shape
    width = mine.shape[1]
    rel_rows = (depth - 4 * mine.shape[0]) // 3
    args = (mine, theirs, cat, rel)
    return pl.pallas_call(
        functools.partial(forward_kernel, block, rel.shape[0]),
        grid_spec=pltpu.PrefetchScalarGridSpec(
            num_scalar_prefetch=1,
            grid=(1,),
            in_specs=[fixed(x.shape) for x in args[:3]] + [fixed((rel_rows, width))],
            out_specs=[fixed((rows, width)), fixed((rows, width))],
            scratch_shapes=[pltpu.VMEM((depth, width), BF)],
        ),
        out_shape=shaped(((rows, width), F32), ((rows, width), BF)),
        compiler_params=params(mine.shape[0] <= 512, 16),
        name="forward_partial",
    )(core, *args)


def activate_kernel(planes, flips, cut, plane, grp, win_ref, wself_ref, *refs):
    agg_pieces = refs[: planes * flips]
    sources = refs[planes * flips : planes * flips + 6]
    outs = refs[planes * flips + 6 : planes * flips + 10]
    *held, sems = refs[planes * flips + 10 :]
    agg_ref, node_ref, h_ref, d_ref = held
    rows = sources[0].shape[0]
    block = rows // flips
    for s in range(planes):
        j = lax.rem(plane[0] - s + planes, planes)
        for a in range(flips):
            at = rows_at(j * flips + (grp[0] ^ a), block)
            agg_ref[at, :] = agg_pieces[s * flips + a][...]
            if s > 0:
                which, row = stacked(s, a, cut, block)
                node_ref[at, :] = sources[which][row : row + block, :]
        if s == 0:
            node_ref[rows_at(j, rows), :] = sources[0][...]

    def embed(j, carry):
        at = rows_at(j, rows)
        act = jnp.tanh(dot(agg_ref[at, :], win_ref[...]) + dot(node_ref[at, :], wself_ref[...]))
        h_ref[at, :] = act.astype(BF)
        d_ref[at, :] = (1.0 - act * act).astype(BF)
        for n in range(4):
            pltpu.make_async_copy(held[n].at[at, :], outs[n].at[at, :], sems.at[n, j]).start()
        return carry

    def finish(j, carry):
        at = rows_at(j, rows)
        for n in range(4):
            pltpu.make_async_copy(held[n].at[at, :], outs[n].at[at, :], sems.at[n, j]).wait()
        return carry

    lax.fori_loop(0, planes, embed, 0)
    lax.fori_loop(0, planes, finish, 0)


def activate(plane, grp, agg_pieces, sources, w_in, w_self):
    rows, width = sources[0].shape
    block = agg_pieces[0].shape[0]
    flips = rows // block
    cut = 1 + sources[4].shape[0] // block
    planes = len(agg_pieces) // flips
    out = ((planes * rows, width), BF)
    args = (w_in, w_self, *agg_pieces, *sources)
    return pl.pallas_call(
        functools.partial(activate_kernel, planes, flips, cut),
        grid_spec=pltpu.PrefetchScalarGridSpec(
            num_scalar_prefetch=2,
            grid=(1,),
            in_specs=[fixed(x.shape) for x in args],
            out_specs=[pl.BlockSpec(memory_space=pl.ANY)] * 4,
            scratch_shapes=[pltpu.VMEM(*out)] * 4 + [pltpu.SemaphoreType.DMA((4, planes))],
        ),
        out_shape=shaped(*[out] * 4),
        compiler_params=params(planes <= 4, 60),
        name="activate",
    )(plane, grp, *args)


def row_gradient(gs, h, start, qb_ref, qg_ref, meta_ref):
    step, width = h.shape
    count = qb_ref.shape[0]
    colsum = dot(gs, jnp.ones((count, 128), BF))
    colsum = jnp.concatenate([colsum] * (width // 128), axis=1)
    row = lax.broadcasted_iota(I32, (step, count), 0)
    picked = jnp.where(row == meta_ref[8:9, :] - start, 1.0, 0.0).astype(BF)
    grad = dot(gs, qb_ref[...]) - h.astype(F32) * colsum
    return 2.0 * width ** (-0.5) * grad + dot(picked, qg_ref[...])


def score_kernel(block, step, total_q, own_ref, other_ref, rel_ref, bias_ref, meta_ref, *refs):
    gs_ref, qg_ref, qb_ref, loss_ref = refs[:4]
    s_ref, ht_ref = refs[-2:]
    half, width = own_ref.shape
    qt = rel_ref.shape[0]
    scale = width ** (-0.5)
    blocks = step // block
    halves = ((0, own_ref), (half, other_ref))
    tail = meta_ref[0:1, :]
    head = jnp.broadcast_to(meta_ref[8:9, :].astype(F32), (128, qt)).T
    head = jnp.concatenate([head] * (step // 128), axis=1).astype(I32)

    q = rel_ref[...]
    for base, ref in halves:

        def pick(b, q):
            column = lax.broadcasted_iota(I32, (qt, step), 1)
            picked = jnp.where(column == head - (base + b * step), 1.0, 0.0).astype(BF)
            return q + dot(picked, ref[rows_at(b, step), :])

        q = lax.fori_loop(0, half // step, pick, q)
    qb_ref[...] = q.astype(BF)
    flipped = q.T
    hi, lo = split(flipped * (2.0 * scale))
    qsq = scale * jnp.sum(flipped * flipped, axis=0, keepdims=True)

    top = jnp.full((8, qt), 2.0 * NEG_FILL, F32)
    for base, ref in halves:

        def first(b, top):
            hb = ref[rows_at(b, step), :]
            cross = dot(hb, hi) + dot(hb, lo)
            x = hb.astype(F32)
            hsq = scale * jnp.sum(x * x, axis=1, keepdims=True)
            ht_ref[:, pl.ds(pl.multiple_of(base + b * step, step), step)] = x.T.astype(BF)
            for u in range(blocks):
                at = slice(u * block, (u + 1) * block)
                bias = bias_ref[pl.ds(base // block + b * blocks + u, 1), :] - qsq
                s = cross[at] - hsq[at] + bias
                s_ref[pl.ds(pl.multiple_of(base + b * step + u * block, block), block), :] = s
                top = jnp.maximum(top, jnp.max(s.reshape(block // 8, 8, qt), axis=0))
            return top

        top = lax.fori_loop(0, half // step, first, top, unroll=2)
    top = jnp.max(top, axis=0, keepdims=True)
    row = lax.broadcasted_iota(I32, (block, qt), 0)

    def second(b, carry):
        norm, truth = carry
        s = s_ref[rows_at(b, block), :]
        e = jnp.exp(s - top)
        s_ref[rows_at(b, block), :] = e
        at_tail = jnp.where(row == tail - b * block, s, 0.0)
        norm = norm + jnp.sum(e.reshape(block // 8, 8, qt), axis=0)
        truth = truth + jnp.sum(at_tail.reshape(block // 8, 8, qt), axis=0)
        return norm, truth

    zero = jnp.zeros((8, qt), F32)
    norm, truth = lax.fori_loop(0, 2 * half // block, second, (zero, zero))
    norm = jnp.sum(norm, axis=0, keepdims=True)
    truth = jnp.sum(truth, axis=0, keepdims=True)
    loss_ref[...] = top + jnp.log(norm) - truth
    inverse = 1.0 / norm
    share = inverse * (1.0 / total_q)

    def third(b, carry):
        picked = jnp.where(row == tail - b * block, 1.0 / total_q, 0.0)
        gs_ref[rows_at(b, block), :] = (s_ref[rows_at(b, block), :] * share - picked).astype(BF)
        return carry

    lax.fori_loop(0, 2 * half // block, third, 0)
    pulled = dot(ht_ref[...], gs_ref[...])
    rowsum = (norm * inverse - 1.0) * (1.0 / total_q)
    qg_ref[...] = (2.0 * scale * (pulled - flipped * rowsum)).T.astype(BF)
    for grad_ref in refs[4:-2]:

        def push(b, carry):
            at = pl.ds(pl.multiple_of(half + b * step, step), step)
            grad = row_gradient(
                gs_ref[at, :], other_ref[rows_at(b, step), :], half + b * step, qb_ref, qg_ref, meta_ref
            )
            grad_ref[rows_at(b, step), :] = grad.astype(BF)
            return carry

        lax.fori_loop(0, half // step, push, 0)


def score(own, other, rel, bias, meta, block, total_q):
    half, width = own.shape
    total = 2 * half
    count = rel.shape[0]
    whole = total * count <= 4096 * 512
    qt = count if whole else 128
    once = dict(pipeline_mode=pl.Buffered(1)) if whole else {}
    wide = pl.BlockSpec((qt, width), lambda i: (i, 0), **once)
    return pl.pallas_call(
        functools.partial(score_kernel, block, min(512, half), total_q),
        grid=(count // qt,),
        in_specs=[
            fixed(own.shape),
            fixed(other.shape),
            wide,
            pl.BlockSpec((bias.shape[0], qt), lambda i: (0, i), **once),
            pl.BlockSpec((meta.shape[0], qt), lambda i: (0, i), **once),
        ],
        out_specs=[
            pl.BlockSpec((total, qt), lambda i: (0, i), **once),
            wide,
            wide,
            pl.BlockSpec((1, qt), lambda i: (0, i), **once),
        ]
        + [fixed(other.shape)] * whole,
        out_shape=shaped(
            ((total, count), BF),
            ((count, width), BF),
            ((count, width), BF),
            ((1, count), F32),
            *[(other.shape, BF)] * whole,
        ),
        scratch_shapes=[pltpu.VMEM((total, qt), F32), pltpu.VMEM((width, total), BF)],
        compiler_params=params(whole, 28),
        cost_estimate=cost(60),
        name="score",
    )(own, other, rel, bias, meta)


def rows_kernel(base, gs_ref, qb_ref, qg_ref, meta_ref, h_ref, out_ref):
    start = base + pl.program_id(0) * h_ref.shape[0]
    grad = row_gradient(gs_ref[...], h_ref[...], start, qb_ref, qg_ref, meta_ref)
    out_ref[...] = grad.astype(BF)


def rows(base, gs, qb, qg, meta, h, name):
    half, width = h.shape
    count = qb.shape[0]
    step = min(512, half)
    tall = pl.BlockSpec((step, width), lambda i: (i, 0))
    return pl.pallas_call(
        functools.partial(rows_kernel, base),
        grid=(half // step,),
        in_specs=[
            pl.BlockSpec((step, count), lambda i: (i + base // step, 0)),
            fixed(qb.shape),
            fixed(qg.shape),
            fixed(meta.shape),
            tall,
        ],
        out_specs=tall,
        out_shape=jax.ShapeDtypeStruct((half, width), BF),
        compiler_params=params(half <= 2048, 10),
        cost_estimate=cost(0),
        name=name,
    )(gs, qb, qg, meta, h)


def backward_kernel(tiles, block, planes, plane, own_ref, other_ref, d_ref, win_ref, send_ref, *refs):
    got = refs[: planes - 1]
    pre_ref, agg_grad_ref, mine_ref, theirs_ref, owned, box, sems = refs[planes - 1 :]
    j = pl.program_id(0)
    part_rows = block + MARK_ROWS
    used = 2 * part_rows

    @pl.when(j == 0)
    def _():
        owned[...] = jnp.zeros_like(owned)
        for s in range(planes):
            at = lax.rem(plane[0] - s + planes, planes)
            source = send_ref.at[plane[0]] if s == 0 else got[s - 1]
            pltpu.make_async_copy(source.at[0:used, :], box.at[at], sems.at[at]).start()

    pltpu.make_async_copy(send_ref.at[0, 0:used, :], box.at[j], sems.at[j]).wait()
    grad = own_ref[...].astype(F32) + other_ref[...].astype(F32)
    pre = (grad * d_ref[...].astype(F32)).astype(BF)
    pre_ref[...] = pre
    agg_grad = dot_nt(pre, win_ref[...]).astype(BF)
    agg_grad_ref[...] = agg_grad
    back = dot(box[j], agg_grad)
    for s in range(2):
        part = back[s * part_rows : s * part_rows + block]
        which = box[j, s * part_rows + block : (s + 1) * part_rows, :].astype(F32)[0:1, 0:1]
        for t in range(tiles):
            owned[s * tiles + t] = owned[s * tiles + t] + jnp.where(which == t, part, 0.0)

    @pl.when(j == pl.num_programs(0) - 1)
    def _():
        for t in range(tiles):
            mine_ref[t * block : (t + 1) * block, :] = owned[t]
            theirs_ref[t * block : (t + 1) * block, :] = owned[tiles + t].astype(BF)


def backward(plane, own, other, d, w_in, send, got, tiles, block):
    half, width = own.shape
    planes, _, node_rows = send.shape
    tall = pl.BlockSpec((node_rows, width), lambda i, plane: (i, 0))
    anywhere = pl.BlockSpec(memory_space=pl.ANY)
    return pl.pallas_call(
        functools.partial(backward_kernel, tiles, block, planes),
        grid_spec=pltpu.PrefetchScalarGridSpec(
            num_scalar_prefetch=1,
            grid=(planes,),
            in_specs=[tall] * 3 + [fixed(w_in.shape)] + [anywhere] * planes,
            out_specs=[tall, tall] + [fixed((node_rows, width))] * 2,
            scratch_shapes=[
                pltpu.VMEM((2 * tiles, block, width), F32),
                pltpu.VMEM((planes, 2 * (block + MARK_ROWS), node_rows), BF),
                pltpu.SemaphoreType.DMA((planes,)),
            ],
        ),
        out_shape=shaped(
            ((half, width), BF),
            ((half, width), BF),
            ((node_rows, width), F32),
            ((node_rows, width), BF),
        ),
        compiler_params=params(planes <= 4, 16),
        cost_estimate=cost(6),
        name="backward_rows",
    )(plane, own, other, d, w_in, send, *got)


def sums_kernel(skip, planes, plane, pre_ref, agg_ref, node_ref, agg_grad_ref, send_ref, *refs):
    got = refs[: planes - 1]
    out_ref, gw, grel, box, sems = refs[planes - 1 :]
    j = pl.program_id(0)
    node_rows, width = pre_ref.shape
    used = box.shape[1]

    @pl.when(j == 0)
    def _():
        gw[...] = jnp.zeros_like(gw)
        grel[...] = jnp.zeros_like(grel)
        for s in range(planes):
            at = lax.rem(plane[0] - s + planes, planes)
            source = send_ref.at[plane[0]] if s == 0 else got[s - 1]
            pltpu.make_async_copy(source.at[skip : skip + used, :], box.at[at], sems.at[at]).start()

    pltpu.make_async_copy(send_ref.at[0, skip : skip + used, :], box.at[j], sems.at[j]).wait()
    quarter = used // 2
    tiles = node_rows // 128
    cut = [slice(t * 128, (t + 1) * 128) for t in range(tiles)]
    line = jnp.concatenate([box[j, 0:quarter, at] for at in cut], axis=0)
    ids = jnp.concatenate([box[j, quarter:, at] for at in cut], axis=0).astype(F32)
    spread = jnp.concatenate(
        [jnp.where(ids[:, 64:65] == t, line.astype(F32), 0.0) for t in range(tiles)], axis=1
    ).astype(BF)
    pulled = dot(spread, agg_grad_ref[...])
    hi, lo = split(pulled)
    flat = jnp.broadcast_to(ids[:, 0:1], (tiles * quarter, 128)).T[0:1, :]
    relation = lax.broadcasted_iota(I32, (grel.shape[0], tiles * quarter), 0).astype(F32)
    chosen = jnp.where(relation == flat, 1.0, 0.0).astype(BF)
    grel[...] = grel[...] - (dot(chosen, hi) + dot(chosen, lo))
    flipped = pre_ref[...].astype(F32).T.astype(BF)
    gw[0] = gw[0] + dot(flipped, agg_ref[...])
    gw[1] = gw[1] + dot(flipped, node_ref[...])

    @pl.when(j == pl.num_programs(0) - 1)
    def _():
        out_ref[0:width, :] = gw[0].T.astype(BF)
        out_ref[width : 2 * width, :] = gw[1].T.astype(BF)
        out_ref[2 * width :, :] = grel[...].astype(BF)


def sums_of_half(plane, pre, agg, nodes, agg_grad, send, got, skip, rel_rows):
    width = pre.shape[1]
    planes, send_rows, node_rows = send.shape
    tall = pl.BlockSpec((node_rows, width), lambda i, plane: (i, 0))
    anywhere = pl.BlockSpec(memory_space=pl.ANY)
    out = ((2 * width + rel_rows, width), BF)
    return pl.pallas_call(
        functools.partial(sums_kernel, skip, planes),
        grid_spec=pltpu.PrefetchScalarGridSpec(
            num_scalar_prefetch=1,
            grid=(planes,),
            in_specs=[tall] * 4 + [anywhere] * planes,
            out_specs=fixed(out[0]),
            scratch_shapes=[
                pltpu.VMEM((2, width, width), F32),
                pltpu.VMEM((rel_rows, width), F32),
                pltpu.VMEM((planes, send_rows - skip, node_rows), BF),
                pltpu.SemaphoreType.DMA((planes,)),
            ],
        ),
        out_shape=shaped(out)[0],
        compiler_params=params(planes <= 4, 16),
        cost_estimate=cost(8),
        name="sums_of_half",
    )(plane, pre, agg, nodes, agg_grad, send, *got)


def shift_planes(x, by, cand_count):
    return lax.ppermute(x, "cand", [(i, (i + 2 * by) % cand_count) for i in range(cand_count)])


def swap_core(x, cand_count):
    return lax.ppermute(x, "cand", [(i, i ^ 1) for i in range(cand_count)])


def swap_grp(x, flip, grp_count):
    return lax.ppermute(x, "grp", [(i, i ^ flip) for i in range(grp_count)])


def total_kernel(a_ref, b_ref, gwin_ref, gwself_ref, grel_ref):
    start = 0
    for ref in (gwin_ref, gwself_ref, grel_ref):
        at = slice(start, start + ref.shape[0])
        ref[...] = a_ref[at, :].astype(F32) + b_ref[at, :].astype(F32)
        start += ref.shape[0]


def total_sums(a, b, rel_count):
    width = a.shape[1]
    outs = [((n, width), F32) for n in (width, width, rel_count)]
    return pl.pallas_call(
        total_kernel,
        in_specs=[pl.BlockSpec(memory_space=pltpu.VMEM)] * 2,
        out_specs=[pl.BlockSpec(memory_space=pltpu.VMEM)] * 3,
        out_shape=shaped(*outs),
        compiler_params=params(True, 12),
        name="total_sums",
    )(a, b)


def gather_planes(x, cand_count):
    return [x] + [shift_planes(x, s, cand_count) for s in range(1, cand_count // 2)]


def gather_stacks(planes, grp_count):
    block = planes[0].shape[0]
    here = jnp.concatenate(planes)
    one, two = swap_grp(here, 1, grp_count), swap_grp(here, 2, grp_count)
    cut = len(planes) // 2 * block
    return [
        here,
        one,
        two,
        swap_grp(one[:cut], 2, grp_count),
        swap_grp(two[cut:], 1, grp_count),
    ]


def gather_pieces(planes, first, cand_count, grp_count):
    pieces = []
    for s in range(first, cand_count // 2):
        found = [planes[s]]
        for flip in range(1, grp_count):
            low, high = flip & -flip, flip - (flip & -flip)
            if high == 0:
                found.append(swap_grp(planes[s], flip, grp_count))
            elif s % 2:
                found.append(swap_grp(found[low], high, grp_count))
            else:
                found.append(swap_grp(found[high], low, grp_count))
        pieces += found
    return pieces


def sum_over_grp(whole, whole_bf, grp_index, grp_count, share_rows):
    total = lax.dynamic_slice_in_dim(whole, grp_index * share_rows, share_rows, 0)
    for flip in range(1, grp_count):
        part = lax.dynamic_slice_in_dim(whole_bf, (grp_index ^ flip) * share_rows, share_rows, 0)
        total = total + swap_grp(part, flip, grp_count).astype(F32)
    return total


def body(
    node_emb,
    rel_emb,
    w_in,
    w_self,
    rel_score,
    mirror_blocks,
    adj_values,
    adj_source,
    adj_target,
    adj_relation,
    live_blocks,
    query_head,
    query_rel,
    allowed,
    true_tail,
):
    cand_count = lax.axis_size("cand")
    grp_count = lax.axis_size("grp")
    grp_index = lax.axis_index("grp").astype(I32)
    cand_index = lax.axis_index("cand").astype(I32)
    nodes = node_emb[0]
    node_rows, width = nodes.shape
    block = adj_values.shape[-1]
    tiles = node_rows // block
    share_rows = node_rows // grp_count
    plane_count = cand_count // 2
    plane, core = cand_index // 2, cand_index % 2
    half = plane_count * node_rows
    want = mirror_blocks.reshape(-1)
    total_q = query_head.shape[0]
    half_q = total_q // 2
    rel_rows = -(-rel_emb.shape[0] // 128) * 128

    own_share = lax.dynamic_slice_in_dim(nodes, grp_index * share_rows, share_rows, 0)
    their_want = swap_core(want, cand_count)
    nodes_at = gather_stacks(gather_planes(own_share, cand_count)[1:], grp_count)
    hold, nodes_at[0] = lax.optimization_barrier((core[None], nodes_at[0]))
    cat, send = fold(
        adj_values[0, 0],
        adj_source[0, 0],
        adj_target[0, 0],
        adj_relation[0, 0],
        live_blocks[0],
        want,
        hold,
        tiles,
        rel_rows,
    )
    mine = jnp.take(want.reshape(plane_count, 2), core, axis=1)
    theirs = jnp.take(their_want.reshape(plane_count, 2), core, axis=1)
    *nodes_at, cat, send = lax.optimization_barrier((nodes, *nodes_at, cat, send))
    mine, theirs = pick(plane[None], grp_index[None], mine, theirs, nodes_at, block)
    theirs = swap_core(theirs, cand_count)
    partial, partial_bf = forward(core[None], mine, theirs, cat, rel_emb, block)
    own_agg = sum_over_grp(partial, partial_bf, grp_index, grp_count, share_rows).astype(BF)
    agg_planes = gather_planes(own_agg, cand_count)
    agg_pieces = gather_pieces(agg_planes, 0, cand_count, grp_count)

    def own_half(x):
        return lax.dynamic_slice_in_dim(x, core * half_q, half_q, 0)

    def order(ids):
        cand = ids // node_rows
        return ((cand % 2) ^ core) * half + (cand // 2) * node_rows + ids % node_rows

    rel_q = jnp.take(rel_score, own_half(query_rel), axis=0)
    allowed_at = order(own_half(allowed) * block) // block
    block_ids = jnp.arange(2 * half // block, dtype=I32)
    hit = jnp.any(allowed_at.T[:, None, :] == block_ids[None, :, None], axis=0)
    bias = jnp.where(hit, 0.0, NEG_FILL).astype(F32)
    meta = jnp.concatenate(
        [
            jnp.broadcast_to(order(own_half(true_tail))[None], (8, half_q)),
            jnp.broadcast_to(order(own_half(query_head))[None], (8, half_q)),
        ]
    )
    agg_pieces, rel_q, bias, meta = lax.optimization_barrier((agg_pieces, rel_q, bias, meta))
    half_agg, half_nodes, half_h, half_d = activate(
        plane[None], grp_index[None], agg_pieces, nodes_at, w_in, w_self
    )

    other_h = swap_core(half_h, cand_count)
    send, half_h = lax.optimization_barrier((send, half_h))
    got = [
        shift_planes(
            lax.dynamic_index_in_dim(send, (plane + s) % plane_count, 0, keepdims=False),
            s,
            cand_count,
        )
        for s in range(1, plane_count)
    ]
    gs, qg, qb, loss, *out_grad = score(half_h, other_h, rel_q, bias, meta, block, total_q)
    gs, *more = lax.optimization_barrier((gs, *out_grad, *got))
    out_grad, got = more[: len(out_grad)], more[len(out_grad) :]
    other_loss = swap_core(loss, cand_count)
    loss = jnp.where(
        core == 0,
        jnp.concatenate([loss[0], other_loss[0]]),
        jnp.concatenate([other_loss[0], loss[0]]),
    )
    out_grad = out_grad[0] if out_grad else rows(half, gs, qb, qg, meta, other_h, "rows_other")
    in_grad = swap_core(out_grad, cand_count)
    own_grad = rows(0, gs, qb, qg, meta, half_h, "rows_own")
    pre, agg_grad, mine, theirs = backward(
        plane[None], own_grad, in_grad, half_d, w_in, send, got, tiles, block
    )
    mine = mine + swap_core(theirs, cand_count).astype(F32)
    mine, pre, agg_grad = lax.optimization_barrier((mine, pre, agg_grad))
    node_grad = sum_over_grp(mine, mine.astype(BF), grp_index, grp_count, share_rows)
    sums = sums_of_half(
        plane[None],
        pre,
        half_agg,
        half_nodes,
        agg_grad,
        send,
        got,
        2 * (block + MARK_ROWS),
        rel_rows,
    )
    gwin, gwself, grel = total_sums(sums, swap_core(sums, cand_count), rel_emb.shape[0])
    first_row = plane * node_rows + grp_index * share_rows
    own_pre = lax.dynamic_slice_in_dim(pre, first_row, share_rows, 0)
    node_grad = node_grad + dot_nt(own_pre, w_self)
    h_own = lax.dynamic_slice_in_dim(half_h, first_row, share_rows, 0)
    return (
        h_own[None],
        loss,
        node_grad[None],
        grel,
        gwin,
        gwself,
    )


def solution(mesh):
    return jax.shard_map(
        body,
        mesh=mesh,
        in_specs=(
            P("cand", None, None),
            P("grp", None),
            P(),
            P(),
            P(),
            P("grp", "cand", None, None),
            P("grp", "cand", None, None, None),
            P("grp", "cand", None),
            P("grp", "cand", None),
            P("grp", "cand", None),
            P("grp", "cand"),
            P(),
            P(),
            P(),
            P(),
        ),
        out_specs=(P("cand", "grp", None), P(), P("cand", "grp", None), P("grp", None), P(), P()),
        check_vma=False,
    )
```

```python
import functools

import jax
import jax.numpy as jnp
from jax import lax
from jax.experimental import pallas as pl
from jax.experimental.pallas import tpu as pltpu
from jax.sharding import PartitionSpec as P

NEG_FILL = -1e30
BF = jnp.bfloat16
F32 = jnp.float32
I32 = jnp.int32
INFO_ROWS = 16


def dot(a, b):
    return jnp.dot(a, b, preferred_element_type=F32)


def dot_nt(a, b):
    return lax.dot_general(a, b, (((1,), (1,)), ((), ())), preferred_element_type=F32)


def split(x):
    hi = x.astype(BF)
    return hi, (x - hi.astype(F32)).astype(BF)


def params(small, mebibytes):
    return pltpu.CompilerParams(vmem_limit_bytes=(mebibytes if small else 60) * 1024 * 1024)


def fixed(shape):
    return pl.BlockSpec(shape, lambda *a: (0,) * len(shape), pipeline_mode=pl.Buffered(1))


def shaped(*pairs):
    return [jax.ShapeDtypeStruct(s, d) for s, d in pairs]


def cost(micros):
    return pl.CostEstimate(flops=micros * 10**9, bytes_accessed=micros * 10**6, transcendentals=0)


def rows_at(index, size):
    return pl.ds(pl.multiple_of(index * size, size), size)


def fold_kernel(tiles, per, src, tgt, rel, live, want, core, a_ref, info_ref, *refs):
    cat_ref, send_ref, acc, wacc, line = refs
    step = pl.program_id(0)
    block = a_ref.shape[1]
    slots = want.shape[0]
    rel_rows = (wacc.shape[0] - 8) // tiles
    count = line.shape[0]

    @pl.when(step == 0)
    def _():
        acc[...] = jnp.zeros_like(acc)
        wacc[...] = jnp.zeros_like(wacc)

    sums = dot_nt(jnp.ones((8, block), BF), a_ref[...].reshape(per * block, block))
    for i in range(per):
        b = step * per + i
        good = b < live[0]
        at = jnp.where(good, tgt[b] * slots + src[b], tiles * slots)
        acc[at] = acc[at] + a_ref[i].astype(F32)
        row = jnp.where(good, tgt[b] * rel_rows + rel[b], tiles * rel_rows)
        total = sums[0:1, i * block : (i + 1) * block]
        wacc[pl.ds(row, 1), :] = wacc[pl.ds(row, 1), :] + total
        line[pl.ds(b, 1), :] = jnp.where(good, total, 0.0)

    @pl.when(step == pl.num_programs(0) - 1)
    def _():
        base = 2 * slots * block
        quarter = count // tiles
        tail = 2 * block + INFO_ROWS
        row = lax.broadcasted_iota(I32, info_ref.shape, 0)
        for z in range(slots // 2):
            info = info_ref[...]
            for n in range(2):
                info = jnp.where(row == 2 + n, want[2 * z + (n ^ core[0])].astype(F32), info)
            send_ref[z, 2 * block : tail, :] = info.astype(BF)
            for t in range(tiles):
                those = line[t * quarter : (t + 1) * quarter, :]
                send_ref[z, tail:, t * block : (t + 1) * block] = those.astype(BF)
        for t in range(tiles):
            at = slice(t * block, (t + 1) * block)
            hi, lo = split(-wacc[t * rel_rows : (t + 1) * rel_rows, :].T)
            cat_ref[at, base : base + rel_rows] = hi
            cat_ref[at, base + rel_rows : base + 2 * rel_rows] = hi
            cat_ref[at, base + 2 * rel_rows :] = lo
            for s in range(slots):
                part = acc[t * slots + s]
                hi, lo = split(part)
                cat_ref[at, s * block : (s + 1) * block] = hi
                cat_ref[at, (slots + s) * block : (slots + s + 1) * block] = lo
                send_ref[s // 2, rows_at(s % 2 ^ core[0], block), at] = part.T.astype(BF)


def fold(adj, src, tgt, rel, live, want, core, tiles, rel_rows):
    count, block, _ = adj.shape
    slots = want.shape[0]
    per = next(p for p in (48, 16, 8, 4, 2, 1) if count % p == 0)
    rows = tiles * block
    info = jnp.pad(jnp.stack([rel, tgt]).astype(F32), ((0, INFO_ROWS - 2), (0, rows - count)))
    outs = [
        ((rows, 2 * slots * block + 3 * rel_rows), BF),
        ((slots // 2, 2 * block + INFO_ROWS + count // tiles, rows), BF),
    ]
    return pl.pallas_call(
        functools.partial(fold_kernel, tiles, per),
        grid_spec=pltpu.PrefetchScalarGridSpec(
            num_scalar_prefetch=6,
            grid=(count // per,),
            in_specs=[
                pl.BlockSpec((per, block, block), lambda i, *a: (i, 0, 0)),
                fixed((INFO_ROWS, rows)),
            ],
            out_specs=[fixed(s) for s, _ in outs],
            scratch_shapes=[
                pltpu.VMEM((tiles * slots + 1, block, block), F32),
                pltpu.VMEM((tiles * rel_rows + 8, block), F32),
                pltpu.VMEM((count, block), F32),
            ],
        ),
        out_shape=shaped(*outs),
        compiler_params=params(slots <= 8, 60),
        cost_estimate=cost(8),
        name="fold_adjacency",
    )(src, tgt, rel, live, want, core, adj, info)


def stacked(shift, flip, cut, block):
    if shift == 0:
        return 0, None
    if flip < 3:
        return 1 + flip, (shift - 1) * block
    return (4, (shift - 1) * block) if shift < cut else (5, (shift - cut) * block)


def pick_kernel(planes, block, cut, plane, grp, core, mine, theirs, *refs):
    sources, (mine_ref, theirs_ref, sems) = refs[:-3], refs[-3:]
    flips = sources[0].shape[0] // block
    for wait in (False, True):
        for n, (ids, out_ref) in enumerate(((mine, mine_ref), (theirs, theirs_ref))):
            for s in range(planes):
                j = lax.rem(plane[0] - s + planes, planes)
                tile = ids[2 * j + core[0]]
                for a in range(1 if s == 0 or wait else flips):
                    which, row = stacked(s, a, cut, block)
                    if s == 0:
                        source = sources[0].at[rows_at(tile, block), :]
                    else:
                        source = sources[which].at[row : row + block, :]
                    target = out_ref.at[rows_at(j, block), :]
                    copy = pltpu.make_async_copy(source, target, sems.at[n, s])
                    if wait:
                        copy.wait()
                    elif s == 0:
                        copy.start()
                    else:

                        @pl.when((tile ^ grp[0]) == a)
                        def _():
                            copy.start()


def pick(plane, grp, core, mine, theirs, sources, block):
    planes = mine.shape[0] // 2
    out = ((planes * block, sources[0].shape[1]), BF)
    cut = 1 + sources[4].shape[0] // block
    anywhere = pl.BlockSpec(memory_space=pl.ANY)
    return pl.pallas_call(
        functools.partial(pick_kernel, planes, block, cut),
        grid_spec=pltpu.PrefetchScalarGridSpec(
            num_scalar_prefetch=5,
            grid=(1,),
            in_specs=[anywhere] * len(sources),
            out_specs=[fixed(out[0])] * 2,
            scratch_shapes=[pltpu.SemaphoreType.DMA((2, planes))],
        ),
        out_shape=shaped(out, out),
        compiler_params=params(planes <= 4, 6),
        name="pick_mirrors",
    )(plane, grp, core, mine, theirs, *sources)


def forward_kernel(block, core, grp, mine_ref, theirs_ref, cat_ref, rel_ref, *refs):
    *share_refs, right, total = refs
    depth = 2 * mine_ref.shape[0]
    rel_count = rel_ref.shape[0]
    rel_rows = (right.shape[0] - 2 * depth) // 3
    for j in range(mine_ref.shape[0] // block):
        at = slice(j * block, (j + 1) * block)
        for base in (0, depth // block):
            right[rows_at(base + 2 * j + core[0], block), :] = mine_ref[at, :]
            right[rows_at(base + 2 * j + 1 - core[0], block), :] = theirs_ref[at, :]
    hi, lo = split(rel_ref[...])
    for i, part in enumerate((hi, lo, hi)):
        base = 2 * depth + i * rel_rows
        edge = rel_count // 16 * 16
        right[base + edge : base + rel_rows, :] = jnp.zeros((rel_rows - edge, right.shape[1]), BF)
        right[base : base + rel_count, :] = part
    total[...] = dot(cat_ref[...], right[...])
    put_shares(total, grp[0], share_refs)


def put_shares(total, grp, refs):
    for flip, ref in enumerate(refs):
        ref[...] = total[rows_at(grp ^ flip, ref.shape[0]), :].astype(ref.dtype)


def share_shapes(rows, width, flips):
    return [((rows // flips, width), BF if flip else F32) for flip in range(flips)]


def merge_kernel(grp, mine_ref, theirs_ref, *refs):
    *share_refs, total = refs
    total[...] = mine_ref[...] + theirs_ref[...].astype(F32)
    put_shares(total, grp[0], share_refs)


def merge(grp, mine, theirs, flips):
    outs = share_shapes(*mine.shape, flips)
    return pl.pallas_call(
        merge_kernel,
        grid_spec=pltpu.PrefetchScalarGridSpec(
            num_scalar_prefetch=1,
            grid=(1,),
            in_specs=[fixed(mine.shape), fixed(theirs.shape)],
            out_specs=[fixed(x) for x, _ in outs],
            scratch_shapes=[pltpu.VMEM(mine.shape, F32)],
        ),
        out_shape=shaped(*outs),
        compiler_params=params(True, 8),
        name="merge_cores",
    )(grp, mine, theirs)


def join_kernel(*refs):
    total = refs[0][...]
    for ref in refs[1:-1]:
        total = total + ref[...].astype(F32)
    refs[-1][...] = total.astype(refs[-1].dtype)


def join(parts, dtype):
    return pl.pallas_call(
        join_kernel,
        in_specs=[pl.BlockSpec(memory_space=pltpu.VMEM)] * len(parts),
        out_specs=pl.BlockSpec(memory_space=pltpu.VMEM),
        out_shape=jax.ShapeDtypeStruct(parts[0].shape, dtype),
        compiler_params=params(True, 4),
        name="join_group",
    )(*parts)


def forward(core, grp, mine, theirs, cat, rel, block, flips):
    rows, depth = cat.shape
    width = mine.shape[1]
    args = (mine, theirs, cat, rel)
    outs = share_shapes(rows, width, flips)
    return pl.pallas_call(
        functools.partial(forward_kernel, block),
        grid_spec=pltpu.PrefetchScalarGridSpec(
            num_scalar_prefetch=2,
            grid=(1,),
            in_specs=[fixed(x.shape) for x in args],
            out_specs=[fixed(x) for x, _ in outs],
            scratch_shapes=[pltpu.VMEM((depth, width), BF), pltpu.VMEM((rows, width), F32)],
        ),
        out_shape=shaped(*outs),
        compiler_params=params(mine.shape[0] <= 512, 16),
        name="forward_partial",
    )(core, grp, *args)


def activate_kernel(planes, flips, cut, plane, grp, win_ref, wself_ref, *refs):
    agg_pieces = refs[: planes * flips]
    sources = refs[planes * flips : planes * flips + 6]
    outs = refs[planes * flips + 6 : planes * flips + 10]
    *held, sems = refs[planes * flips + 10 :]
    agg_ref, node_ref, h_ref, d_ref = held
    rows = sources[0].shape[0]
    block = rows // flips
    for s in range(planes):
        j = lax.rem(plane[0] - s + planes, planes)
        for a in range(flips):
            at = rows_at(j * flips + (grp[0] ^ a), block)
            agg_ref[at, :] = agg_pieces[s * flips + a][...]
            if s > 0:
                which, row = stacked(s, a, cut, block)
                node_ref[at, :] = sources[which][row : row + block, :]
        if s == 0:
            node_ref[rows_at(j, rows), :] = sources[0][...]

    def embed(j, carry):
        at = rows_at(j, rows)
        act = jnp.tanh(dot(agg_ref[at, :], win_ref[...]) + dot(node_ref[at, :], wself_ref[...]))
        h_ref[at, :] = act.astype(BF)
        d_ref[at, :] = (1.0 - act * act).astype(BF)
        for n in range(4):
            pltpu.make_async_copy(held[n].at[at, :], outs[n].at[at, :], sems.at[n, j]).start()
        return carry

    def finish(j, carry):
        at = rows_at(j, rows)
        for n in range(4):
            pltpu.make_async_copy(held[n].at[at, :], outs[n].at[at, :], sems.at[n, j]).wait()
        return carry

    lax.fori_loop(0, planes, embed, 0)
    lax.fori_loop(0, planes, finish, 0)


def activate(plane, grp, agg_pieces, sources, w_in, w_self):
    rows, width = sources[0].shape
    block = agg_pieces[0].shape[0]
    flips = rows // block
    cut = 1 + sources[4].shape[0] // block
    planes = len(agg_pieces) // flips
    out = ((planes * rows, width), BF)
    args = (w_in, w_self, *agg_pieces, *sources)
    return pl.pallas_call(
        functools.partial(activate_kernel, planes, flips, cut),
        grid_spec=pltpu.PrefetchScalarGridSpec(
            num_scalar_prefetch=2,
            grid=(1,),
            in_specs=[fixed(x.shape) for x in args],
            out_specs=[pl.BlockSpec(memory_space=pl.ANY)] * 4,
            scratch_shapes=[pltpu.VMEM(*out)] * 4 + [pltpu.SemaphoreType.DMA((4, planes))],
        ),
        out_shape=shaped(*[out] * 4),
        compiler_params=params(planes <= 4, 60),
        name="activate",
    )(plane, grp, *args)


def row_gradient(gs, h, start, qb_ref, qg_ref, meta_ref):
    step, width = h.shape
    count = qb_ref.shape[0]
    colsum = dot(gs, jnp.ones((count, 128), BF))
    colsum = jnp.concatenate([colsum] * (width // 128), axis=1)
    row = lax.broadcasted_iota(I32, (step, count), 0)
    picked = jnp.where(row == meta_ref[8:9, :] - start, 1.0, 0.0).astype(BF)
    grad = dot(gs, qb_ref[...]) - h.astype(F32) * colsum
    return 2.0 * width ** (-0.5) * grad + dot(picked, qg_ref[...])


def score_kernel(block, step, total_q, own_ref, other_ref, rel_ref, bias_ref, meta_ref, *refs):
    gs_ref, qg_ref, qb_ref, loss_ref = refs[:4]
    s_ref, ht_ref = refs[-2:]
    half, width = own_ref.shape
    qt = rel_ref.shape[0]
    scale = width ** (-0.5)
    blocks = step // block
    halves = ((0, own_ref), (half, other_ref))
    tail = meta_ref[0:1, :]
    head = jnp.broadcast_to(meta_ref[8:9, :].astype(F32), (128, qt)).T
    head = jnp.concatenate([head] * (step // 128), axis=1).astype(I32)

    q = rel_ref[...]
    for base, ref in halves:

        def pick(b, q):
            column = lax.broadcasted_iota(I32, (qt, step), 1)
            picked = jnp.where(column == head - (base + b * step), 1.0, 0.0).astype(BF)
            return q + dot(picked, ref[rows_at(b, step), :])

        q = lax.fori_loop(0, half // step, pick, q)
    qb_ref[...] = q.astype(BF)
    flipped = q.T
    hi, lo = split(flipped * (2.0 * scale))
    qsq = scale * jnp.sum(flipped * flipped, axis=0, keepdims=True)

    top = jnp.full((8, qt), 2.0 * NEG_FILL, F32)
    for base, ref in halves:

        def first(b, top):
            hb = ref[rows_at(b, step), :]
            cross = dot(hb, hi) + dot(hb, lo)
            x = hb.astype(F32)
            hsq = scale * jnp.sum(x * x, axis=1, keepdims=True)
            ht_ref[:, pl.ds(pl.multiple_of(base + b * step, step), step)] = x.T.astype(BF)
            for u in range(blocks):
                at = slice(u * block, (u + 1) * block)
                bias = bias_ref[pl.ds(base // block + b * blocks + u, 1), :] - qsq
                s = cross[at] - hsq[at] + bias
                s_ref[pl.ds(pl.multiple_of(base + b * step + u * block, block), block), :] = s
                top = jnp.maximum(top, jnp.max(s.reshape(block // 8, 8, qt), axis=0))
            return top

        top = lax.fori_loop(0, half // step, first, top, unroll=2)
    top = jnp.max(top, axis=0, keepdims=True)
    row = lax.broadcasted_iota(I32, (block, qt), 0)

    def second(b, carry):
        norm, truth = carry
        s = s_ref[rows_at(b, block), :]
        e = jnp.exp(s - top)
        s_ref[rows_at(b, block), :] = e
        at_tail = jnp.where(row == tail - b * block, s, 0.0)
        norm = norm + jnp.sum(e.reshape(block // 8, 8, qt), axis=0)
        truth = truth + jnp.sum(at_tail.reshape(block // 8, 8, qt), axis=0)
        return norm, truth

    zero = jnp.zeros((8, qt), F32)
    norm, truth = lax.fori_loop(0, 2 * half // block, second, (zero, zero))
    norm = jnp.sum(norm, axis=0, keepdims=True)
    truth = jnp.sum(truth, axis=0, keepdims=True)
    loss_ref[...] = top + jnp.log(norm) - truth
    inverse = 1.0 / norm
    share = inverse * (1.0 / total_q)

    def third(b, carry):
        picked = jnp.where(row == tail - b * block, 1.0 / total_q, 0.0)
        gs_ref[rows_at(b, block), :] = (s_ref[rows_at(b, block), :] * share - picked).astype(BF)
        return carry

    lax.fori_loop(0, 2 * half // block, third, 0)
    pulled = dot(ht_ref[...], gs_ref[...])
    rowsum = (norm * inverse - 1.0) * (1.0 / total_q)
    qg_ref[...] = (2.0 * scale * (pulled - flipped * rowsum)).T.astype(BF)
    for grad_ref in refs[4:-2]:

        def push(b, carry):
            at = pl.ds(pl.multiple_of(half + b * step, step), step)
            grad = row_gradient(
                gs_ref[at, :], other_ref[rows_at(b, step), :], half + b * step, qb_ref, qg_ref, meta_ref
            )
            grad_ref[rows_at(b, step), :] = grad.astype(BF)
            return carry

        lax.fori_loop(0, half // step, push, 0)


def score(own, other, rel, bias, meta, block, total_q):
    half, width = own.shape
    total = 2 * half
    count = rel.shape[0]
    whole = total * count <= 4096 * 512
    qt = count if whole else 128
    once = dict(pipeline_mode=pl.Buffered(1)) if whole else {}
    wide = pl.BlockSpec((qt, width), lambda i: (i, 0), **once)
    return pl.pallas_call(
        functools.partial(score_kernel, block, min(512, half), total_q),
        grid=(count // qt,),
        in_specs=[
            fixed(own.shape),
            fixed(other.shape),
            wide,
            pl.BlockSpec((bias.shape[0], qt), lambda i: (0, i), **once),
            pl.BlockSpec((meta.shape[0], qt), lambda i: (0, i), **once),
        ],
        out_specs=[
            pl.BlockSpec((total, qt), lambda i: (0, i), **once),
            wide,
            wide,
            pl.BlockSpec((1, qt), lambda i: (0, i), **once),
        ]
        + [fixed(other.shape)] * whole,
        out_shape=shaped(
            ((total, count), BF),
            ((count, width), BF),
            ((count, width), BF),
            ((1, count), F32),
            *[(other.shape, BF)] * whole,
        ),
        scratch_shapes=[pltpu.VMEM((total, qt), F32), pltpu.VMEM((width, total), BF)],
        compiler_params=params(whole, 28),
        cost_estimate=cost(60),
        name="score",
    )(own, other, rel, bias, meta)


def rows_kernel(base, gs_ref, qb_ref, qg_ref, meta_ref, h_ref, out_ref):
    start = base + pl.program_id(0) * h_ref.shape[0]
    grad = row_gradient(gs_ref[...], h_ref[...], start, qb_ref, qg_ref, meta_ref)
    out_ref[...] = grad.astype(BF)


def rows(base, gs, qb, qg, meta, h, name):
    half, width = h.shape
    count = qb.shape[0]
    step = min(512, half)
    tall = pl.BlockSpec((step, width), lambda i: (i, 0))
    return pl.pallas_call(
        functools.partial(rows_kernel, base),
        grid=(half // step,),
        in_specs=[
            pl.BlockSpec((step, count), lambda i: (i + base // step, 0)),
            fixed(qb.shape),
            fixed(qg.shape),
            fixed(meta.shape),
            tall,
        ],
        out_specs=tall,
        out_shape=jax.ShapeDtypeStruct((half, width), BF),
        compiler_params=params(half <= 2048, 10),
        cost_estimate=cost(0),
        name=name,
    )(gs, qb, qg, meta, h)


def backward_kernel(tiles, block, planes, plane, grp, own_ref, other_ref, d_ref, *refs):
    win_ref, wself_ref, send_ref, *refs = refs
    got = refs[: planes - 1]
    pre_ref, agg_grad_ref, mine_ref, theirs_ref, self_ref, owned, box, sems = refs[planes - 1 :]
    j = pl.program_id(0)
    used = 2 * block + INFO_ROWS

    @pl.when(j == 0)
    def _():
        owned[...] = jnp.zeros_like(owned)
        for s in range(planes):
            at = lax.rem(plane[0] - s + planes, planes)
            source = send_ref.at[plane[0]] if s == 0 else got[s - 1]
            pltpu.make_async_copy(source.at[0:used, :], box.at[at], sems.at[at]).start()

    pltpu.make_async_copy(send_ref.at[0, 0:used, :], box.at[j], sems.at[j]).wait()
    grad = own_ref[...].astype(F32) + other_ref[...].astype(F32)
    pre = (grad * d_ref[...].astype(F32)).astype(BF)
    pre_ref[...] = pre

    @pl.when(j == plane[0])
    def _():
        self_ref[...] = dot_nt(pre_ref[rows_at(grp[0], block), :], wself_ref[...])

    agg_grad = dot_nt(pre, win_ref[...]).astype(BF)
    agg_grad_ref[...] = agg_grad
    back = dot(box[j, 0 : 2 * block, :], agg_grad)
    info = box[j, 2 * block :, :].astype(F32)
    for s in range(2):
        part = back[s * block : (s + 1) * block]
        which = info[2 + s : 3 + s, 0:1]
        for t in range(tiles):
            owned[s * tiles + t] = owned[s * tiles + t] + jnp.where(which == t, part, 0.0)

    @pl.when(j == pl.num_programs(0) - 1)
    def _():
        for t in range(tiles):
            mine_ref[t * block : (t + 1) * block, :] = owned[t]
            theirs_ref[t * block : (t + 1) * block, :] = owned[tiles + t].astype(BF)


def backward(plane, grp, own, other, d, w_in, w_self, send, got, tiles, block):
    half, width = own.shape
    planes, _, node_rows = send.shape
    tall = pl.BlockSpec((node_rows, width), lambda i, *a: (i, 0))
    anywhere = pl.BlockSpec(memory_space=pl.ANY)
    return pl.pallas_call(
        functools.partial(backward_kernel, tiles, block, planes),
        grid_spec=pltpu.PrefetchScalarGridSpec(
            num_scalar_prefetch=2,
            grid=(planes,),
            in_specs=[tall] * 3 + [fixed(w_in.shape)] * 2 + [anywhere] * planes,
            out_specs=[tall, tall] + [fixed((node_rows, width))] * 2 + [fixed((block, width))],
            scratch_shapes=[
                pltpu.VMEM((2 * tiles, block, width), F32),
                pltpu.VMEM((planes, 2 * block + INFO_ROWS, node_rows), BF),
                pltpu.SemaphoreType.DMA((planes,)),
            ],
        ),
        out_shape=shaped(
            ((half, width), BF),
            ((half, width), BF),
            ((node_rows, width), F32),
            ((node_rows, width), BF),
            ((block, width), F32),
        ),
        compiler_params=params(planes <= 4, 16),
        cost_estimate=cost(6),
        name="backward_rows",
    )(plane, grp, own, other, d, w_in, w_self, send, *got)


def sums_kernel(skip, planes, plane, pre_ref, agg_ref, node_ref, agg_grad_ref, send_ref, *refs):
    got = refs[: planes - 1]
    out_ref, gw, grel, box, sems = refs[planes - 1 :]
    j = pl.program_id(0)
    node_rows, width = pre_ref.shape
    used = box.shape[1]

    @pl.when(j == 0)
    def _():
        gw[...] = jnp.zeros_like(gw)
        grel[...] = jnp.zeros_like(grel)
        for s in range(planes):
            at = lax.rem(plane[0] - s + planes, planes)
            source = send_ref.at[plane[0]] if s == 0 else got[s - 1]
            pltpu.make_async_copy(source.at[skip : skip + used, :], box.at[at], sems.at[at]).start()

    pltpu.make_async_copy(send_ref.at[0, skip : skip + used, :], box.at[j], sems.at[j]).wait()
    quarter = used - INFO_ROWS
    tiles = node_rows // 128
    count = tiles * quarter
    cut = [slice(t * 128, (t + 1) * 128) for t in range(tiles)]
    line = jnp.concatenate([box[j, INFO_ROWS:, at] for at in cut], axis=0).astype(F32)
    info = box[j, 0:INFO_ROWS, :].astype(F32)
    target = jnp.broadcast_to(info[1:2, 0:count], (128, count)).T[:, 0:1]
    spread = [jnp.where(target == t, line, 0.0) for t in range(tiles)]
    hi, lo = split(dot(jnp.concatenate(spread, axis=1).astype(BF), agg_grad_ref[...]))
    relation = lax.broadcasted_iota(I32, (grel.shape[0], count), 0).astype(F32)
    chosen = jnp.where(relation == info[0:1, 0:count], 1.0, 0.0).astype(BF)
    grel[...] = grel[...] - (dot(chosen, hi) + dot(chosen, lo))
    flipped = pre_ref[...].astype(F32).T.astype(BF)
    gw[0] = gw[0] + dot(flipped, agg_ref[...])
    gw[1] = gw[1] + dot(flipped, node_ref[...])

    @pl.when(j == pl.num_programs(0) - 1)
    def _():
        out_ref[0:width, :] = gw[0].T.astype(BF)
        out_ref[width : 2 * width, :] = gw[1].T.astype(BF)
        out_ref[2 * width :, :] = grel[...].astype(BF)


def sums_of_half(plane, pre, agg, nodes, agg_grad, send, got, skip, rel_rows):
    width = pre.shape[1]
    planes, send_rows, node_rows = send.shape
    tall = pl.BlockSpec((node_rows, width), lambda i, plane: (i, 0))
    anywhere = pl.BlockSpec(memory_space=pl.ANY)
    out = ((2 * width + rel_rows, width), BF)
    return pl.pallas_call(
        functools.partial(sums_kernel, skip, planes),
        grid_spec=pltpu.PrefetchScalarGridSpec(
            num_scalar_prefetch=1,
            grid=(planes,),
            in_specs=[tall] * 4 + [anywhere] * planes,
            out_specs=fixed(out[0]),
            scratch_shapes=[
                pltpu.VMEM((2, width, width), F32),
                pltpu.VMEM((rel_rows, width), F32),
                pltpu.VMEM((planes, send_rows - skip, node_rows), BF),
                pltpu.SemaphoreType.DMA((planes,)),
            ],
        ),
        out_shape=shaped(out)[0],
        compiler_params=params(planes <= 4, 16),
        cost_estimate=cost(20),
        name="sums_of_half",
    )(plane, pre, agg, nodes, agg_grad, send, *got)


def shift_planes(x, by, cand_count):
    return lax.ppermute(x, "cand", [(i, (i + 2 * by) % cand_count) for i in range(cand_count)])


def swap_core(x, cand_count):
    return lax.ppermute(x, "cand", [(i, i ^ 1) for i in range(cand_count)])


def swap_grp(x, flip, grp_count):
    return lax.ppermute(x, "grp", [(i, i ^ flip) for i in range(grp_count)])


def total_kernel(a_ref, b_ref, gwin_ref, gwself_ref, grel_ref):
    start = 0
    for ref in (gwin_ref, gwself_ref, grel_ref):
        at = slice(start, start + ref.shape[0])
        ref[...] = a_ref[at, :].astype(F32) + b_ref[at, :].astype(F32)
        start += ref.shape[0]


def total_sums(a, b, rel_count):
    width = a.shape[1]
    outs = [((n, width), F32) for n in (width, width, rel_count)]
    return pl.pallas_call(
        total_kernel,
        in_specs=[pl.BlockSpec(memory_space=pltpu.VMEM)] * 2,
        out_specs=[pl.BlockSpec(memory_space=pltpu.VMEM)] * 3,
        out_shape=shaped(*outs),
        compiler_params=params(True, 12),
        name="total_sums",
    )(a, b)


def gather_planes(x, cand_count):
    return [x] + [shift_planes(x, s, cand_count) for s in range(1, cand_count // 2)]


def gather_stacks(here, block, grp_count):
    one, two = swap_grp(here, 1, grp_count), swap_grp(here, 2, grp_count)
    cut = here.shape[0] // block // 2 * block
    return [
        here,
        one,
        two,
        swap_grp(one[:cut], 2, grp_count),
        swap_grp(two[cut:], 1, grp_count),
    ]


def gather_pieces(planes, first, cand_count, grp_count):
    pieces = []
    for s in range(first, cand_count // 2):
        found = [planes[s]]
        for flip in range(1, grp_count):
            low, high = flip & -flip, flip - (flip & -flip)
            if high == 0:
                found.append(swap_grp(planes[s], flip, grp_count))
            elif s % 2:
                found.append(swap_grp(found[low], high, grp_count))
            else:
                found.append(swap_grp(found[high], low, grp_count))
        pieces += found
    return pieces


def swap_shares(parts, grp_count):
    return [swap_grp(part, flip + 1, grp_count) for flip, part in enumerate(parts)]


def body(
    node_emb,
    rel_emb,
    w_in,
    w_self,
    rel_score,
    mirror_blocks,
    adj_values,
    adj_source,
    adj_target,
    adj_relation,
    live_blocks,
    query_head,
    query_rel,
    allowed,
    true_tail,
):
    cand_count = lax.axis_size("cand")
    grp_count = lax.axis_size("grp")
    grp_index = lax.axis_index("grp").astype(I32)
    cand_index = lax.axis_index("cand").astype(I32)
    nodes = node_emb[0]
    node_rows, width = nodes.shape
    block = adj_values.shape[-1]
    tiles = node_rows // block
    share_rows = node_rows // grp_count
    plane_count = cand_count // 2
    plane, core = cand_index // 2, cand_index % 2
    half = plane_count * node_rows
    want = mirror_blocks.reshape(-1)
    total_q = query_head.shape[0]
    half_q = total_q // 2
    rel_rows = -(-rel_emb.shape[0] // 128) * 128

    own_share = lax.dynamic_slice_in_dim(nodes, grp_index * share_rows, share_rows, 0)
    their_want = swap_core(want, cand_count)
    stack = jnp.concatenate(gather_planes(own_share, cand_count)[1:])
    cat, send = fold(
        adj_values[0, 0],
        adj_source[0, 0],
        adj_target[0, 0],
        adj_relation[0, 0],
        live_blocks[0],
        want,
        core[None],
        tiles,
        rel_rows,
    )
    stack, cat, send = lax.optimization_barrier((stack, cat, send))
    nodes_at = [nodes, *gather_stacks(stack, share_rows, grp_count)]

    mine, theirs = pick(
        plane[None], grp_index[None], core[None], want, their_want, nodes_at, block
    )
    theirs = swap_core(theirs, cand_count)
    own, *parts = forward(
        core[None], grp_index[None], mine, theirs, cat, rel_emb, block, grp_count
    )
    own_agg = join([own, *swap_shares(parts, grp_count)], BF)
    agg_planes = gather_planes(own_agg, cand_count)
    agg_pieces = gather_pieces(agg_planes, 0, cand_count, grp_count)

    def own_half(x):
        return lax.dynamic_slice_in_dim(x, core * half_q, half_q, 0)

    def order(ids):
        cand = ids // node_rows
        return ((cand % 2) ^ core) * half + (cand // 2) * node_rows + ids % node_rows

    rel_q = jnp.take(rel_score, own_half(query_rel), axis=0)
    allowed_at = order(own_half(allowed) * block) // block
    block_ids = jnp.arange(2 * half // block, dtype=I32)
    hit = jnp.any(allowed_at.T[:, None, :] == block_ids[None, :, None], axis=0)
    bias = jnp.where(hit, 0.0, NEG_FILL).astype(F32)
    meta = jnp.concatenate(
        [
            jnp.broadcast_to(order(own_half(true_tail))[None], (8, half_q)),
            jnp.broadcast_to(order(own_half(query_head))[None], (8, half_q)),
        ]
    )
    agg_pieces, rel_q, bias, meta = lax.optimization_barrier((agg_pieces, rel_q, bias, meta))
    half_agg, half_nodes, half_h, half_d = activate(
        plane[None], grp_index[None], agg_pieces, nodes_at, w_in, w_self
    )

    other_h = swap_core(half_h, cand_count)

    def send_to_plane(x, by):
        part = lax.dynamic_index_in_dim(x, (plane + by) % plane_count, 0, keepdims=False)
        return shift_planes(part, by, cand_count)

    send_after = lax.optimization_barrier((send, half_h))[0]
    got = [send_to_plane(send_after, by) for by in range(1, plane_count)]
    first_row = plane * node_rows + grp_index * share_rows
    h_own = lax.dynamic_slice_in_dim(half_h, first_row, share_rows, 0)
    other_h, h_own = lax.optimization_barrier((other_h, h_own))
    gs, qg, qb, loss, *out_grad = score(half_h, other_h, rel_q, bias, meta, block, total_q)
    gs, *more = lax.optimization_barrier((gs, *out_grad, *got))
    out_grad, got = more[: len(out_grad)], more[len(out_grad) :]
    other_loss = swap_core(loss, cand_count)
    loss = jnp.where(
        core == 0,
        jnp.concatenate([loss[0], other_loss[0]]),
        jnp.concatenate([other_loss[0], loss[0]]),
    )
    out_grad = out_grad[0] if out_grad else rows(half, gs, qb, qg, meta, other_h, "rows_other")
    in_grad = swap_core(out_grad, cand_count)
    own_grad = rows(0, gs, qb, qg, meta, half_h, "rows_own")
    pre, agg_grad, mine, theirs, self_grad = backward(
        plane[None],
        grp_index[None],
        own_grad,
        in_grad,
        half_d,
        w_in,
        w_self,
        send,
        got,
        tiles,
        block,
    )
    sums = sums_of_half(
        plane[None],
        pre,
        half_agg,
        half_nodes,
        agg_grad,
        send,
        got,
        2 * block,
        rel_rows,
    )
    gwin, gwself, grel = total_sums(sums, swap_core(sums, cand_count), rel_emb.shape[0])
    own, *parts = merge(grp_index[None], mine, swap_core(theirs, cand_count), grp_count)
    own, gwin, gwself, grel = lax.optimization_barrier((own, gwin, gwself, grel))
    node_grad = join([own, self_grad, *swap_shares(parts, grp_count)], F32)
    return (
        h_own[None],
        loss,
        node_grad[None],
        grel,
        gwin,
        gwself,
    )


def solution(mesh):
    return jax.shard_map(
        body,
        mesh=mesh,
        in_specs=(
            P("cand", None, None),
            P("grp", None),
            P(),
            P(),
            P(),
            P("grp", "cand", None, None),
            P("grp", "cand", None, None, None),
            P("grp", "cand", None),
            P("grp", "cand", None),
            P("grp", "cand", None),
            P("grp", "cand"),
            P(),
            P(),
            P(),
            P(),
        ),
        out_specs=(P("cand", "grp", None), P(), P("cand", "grp", None), P("grp", None), P(), P()),
        check_vma=False,
    )
```

```python
import functools

import jax
import jax.numpy as jnp
from jax import lax
from jax.experimental import pallas as pl
from jax.experimental.pallas import tpu as pltpu
from jax.sharding import PartitionSpec as P

NEG_FILL = -1e30
BF = jnp.bfloat16
F32 = jnp.float32
I32 = jnp.int32
INFO_ROWS = 16


def dot(a, b):
    return jnp.dot(a, b, preferred_element_type=F32)


def dot_nt(a, b):
    return lax.dot_general(a, b, (((1,), (1,)), ((), ())), preferred_element_type=F32)


def split(x):
    hi = x.astype(BF)
    return hi, (x - hi.astype(F32)).astype(BF)


def params(small, mebibytes):
    return pltpu.CompilerParams(vmem_limit_bytes=(mebibytes if small else 60) * 1024 * 1024)


def fixed(shape):
    return pl.BlockSpec(shape, lambda *a: (0,) * len(shape), pipeline_mode=pl.Buffered(1))


def shaped(*pairs):
    return [jax.ShapeDtypeStruct(s, d) for s, d in pairs]


def cost(micros):
    return pl.CostEstimate(flops=micros * 10**9, bytes_accessed=micros * 10**6, transcendentals=0)


def rows_at(index, size):
    return pl.ds(pl.multiple_of(index * size, size), size)


def fold_kernel(tiles, per, src, tgt, rel, live, want, core, a_ref, info_ref, *refs):
    cat_ref, send_ref, acc, wacc, line = refs
    step = pl.program_id(0)
    block = a_ref.shape[1]
    slots = want.shape[0]
    rel_rows = (wacc.shape[0] - 8) // tiles
    count = line.shape[0]

    @pl.when(step == 0)
    def _():
        acc[...] = jnp.zeros_like(acc)
        wacc[...] = jnp.zeros_like(wacc)

    sums = dot_nt(jnp.ones((8, block), BF), a_ref[...].reshape(per * block, block))
    for i in range(per):
        b = step * per + i
        good = b < live[0]
        at = jnp.where(good, tgt[b] * slots + src[b], tiles * slots)
        acc[at] = acc[at] + a_ref[i].astype(F32)
        row = jnp.where(good, tgt[b] * rel_rows + rel[b], tiles * rel_rows)
        total = sums[0:1, i * block : (i + 1) * block]
        wacc[pl.ds(row, 1), :] = wacc[pl.ds(row, 1), :] + total
        line[pl.ds(b, 1), :] = jnp.where(good, total, 0.0)

    @pl.when(step == pl.num_programs(0) - 1)
    def _():
        base = 2 * slots * block
        quarter = count // tiles
        tail = 2 * block + INFO_ROWS
        row = lax.broadcasted_iota(I32, info_ref.shape, 0)
        for z in range(slots // 2):
            info = info_ref[...]
            for n in range(2):
                info = jnp.where(row == 2 + n, want[2 * z + (n ^ core[0])].astype(F32), info)
            send_ref[z, 2 * block : tail, :] = info.astype(BF)
            for t in range(tiles):
                those = line[t * quarter : (t + 1) * quarter, :]
                send_ref[z, tail:, t * block : (t + 1) * block] = those.astype(BF)
        for t in range(tiles):
            at = slice(t * block, (t + 1) * block)
            hi, lo = split(-wacc[t * rel_rows : (t + 1) * rel_rows, :].T)
            cat_ref[at, base : base + rel_rows] = hi
            cat_ref[at, base + rel_rows : base + 2 * rel_rows] = hi
            cat_ref[at, base + 2 * rel_rows :] = lo
            for s in range(slots):
                part = acc[t * slots + s]
                hi, lo = split(part)
                cat_ref[at, s * block : (s + 1) * block] = hi
                cat_ref[at, (slots + s) * block : (slots + s + 1) * block] = lo
                send_ref[s // 2, rows_at(s % 2 ^ core[0], block), at] = part.T.astype(BF)


def fold(adj, src, tgt, rel, live, want, core, tiles, rel_rows):
    count, block, _ = adj.shape
    slots = want.shape[0]
    per = next(p for p in (48, 16, 8, 4, 2, 1) if count % p == 0)
    rows = tiles * block
    info = jnp.pad(jnp.stack([rel, tgt]).astype(F32), ((0, INFO_ROWS - 2), (0, rows - count)))
    outs = [
        ((rows, 2 * slots * block + 3 * rel_rows), BF),
        ((slots // 2, 2 * block + INFO_ROWS + count // tiles, rows), BF),
    ]
    return pl.pallas_call(
        functools.partial(fold_kernel, tiles, per),
        grid_spec=pltpu.PrefetchScalarGridSpec(
            num_scalar_prefetch=6,
            grid=(count // per,),
            in_specs=[
                pl.BlockSpec((per, block, block), lambda i, *a: (i, 0, 0)),
                fixed((INFO_ROWS, rows)),
            ],
            out_specs=[fixed(s) for s, _ in outs],
            scratch_shapes=[
                pltpu.VMEM((tiles * slots + 1, block, block), F32),
                pltpu.VMEM((tiles * rel_rows + 8, block), F32),
                pltpu.VMEM((count, block), F32),
            ],
        ),
        out_shape=shaped(*outs),
        compiler_params=params(slots <= 8, 60),
        cost_estimate=cost(8),
        name="fold_adjacency",
    )(src, tgt, rel, live, want, core, adj, info)


def stacked(shift, flip, cut, block):
    if shift == 0:
        return 0, None
    if flip < 3:
        return 1 + flip, (shift - 1) * block
    return (4, (shift - 1) * block) if shift < cut else (5, (shift - cut) * block)


def pick_kernel(planes, block, cut, plane, grp, core, mine, theirs, *refs):
    sources, (mine_ref, theirs_ref, sems) = refs[:-3], refs[-3:]
    flips = sources[0].shape[0] // block
    for wait in (False, True):
        for n, (ids, out_ref) in enumerate(((mine, mine_ref), (theirs, theirs_ref))):
            for s in range(planes):
                j = lax.rem(plane[0] - s + planes, planes)
                tile = ids[2 * j + core[0]]
                for a in range(1 if s == 0 or wait else flips):
                    which, row = stacked(s, a, cut, block)
                    if s == 0:
                        source = sources[0].at[rows_at(tile, block), :]
                    else:
                        source = sources[which].at[row : row + block, :]
                    target = out_ref.at[rows_at(j, block), :]
                    copy = pltpu.make_async_copy(source, target, sems.at[n, s])
                    if wait:
                        copy.wait()
                    elif s == 0:
                        copy.start()
                    else:

                        @pl.when((tile ^ grp[0]) == a)
                        def _():
                            copy.start()


def pick(plane, grp, core, mine, theirs, sources, block):
    planes = mine.shape[0] // 2
    out = ((planes * block, sources[0].shape[1]), BF)
    cut = 1 + sources[4].shape[0] // block
    anywhere = pl.BlockSpec(memory_space=pl.ANY)
    return pl.pallas_call(
        functools.partial(pick_kernel, planes, block, cut),
        grid_spec=pltpu.PrefetchScalarGridSpec(
            num_scalar_prefetch=5,
            grid=(1,),
            in_specs=[anywhere] * len(sources),
            out_specs=[fixed(out[0])] * 2,
            scratch_shapes=[pltpu.SemaphoreType.DMA((2, planes))],
        ),
        out_shape=shaped(out, out),
        compiler_params=params(planes <= 4, 6),
        name="pick_mirrors",
    )(plane, grp, core, mine, theirs, *sources)


def forward_kernel(block, core, grp, mine_ref, theirs_ref, cat_ref, rel_ref, *refs):
    *share_refs, right, total = refs
    depth = 2 * mine_ref.shape[0]
    rel_count = rel_ref.shape[0]
    rel_rows = (right.shape[0] - 2 * depth) // 3
    for j in range(mine_ref.shape[0] // block):
        at = slice(j * block, (j + 1) * block)
        for base in (0, depth // block):
            right[rows_at(base + 2 * j + core[0], block), :] = mine_ref[at, :]
            right[rows_at(base + 2 * j + 1 - core[0], block), :] = theirs_ref[at, :]
    hi, lo = split(rel_ref[...])
    for i, part in enumerate((hi, lo, hi)):
        base = 2 * depth + i * rel_rows
        edge = rel_count // 16 * 16
        right[base + edge : base + rel_rows, :] = jnp.zeros((rel_rows - edge, right.shape[1]), BF)
        right[base : base + rel_count, :] = part
    total[...] = dot(cat_ref[...], right[...])
    put_shares(total, grp[0], share_refs)


def put_shares(total, grp, refs):
    for flip, ref in enumerate(refs):
        ref[...] = total[rows_at(grp ^ flip, ref.shape[0]), :].astype(ref.dtype)


def share_shapes(rows, width, flips):
    return [((rows // flips, width), BF if flip else F32) for flip in range(flips)]


def join_kernel(*refs):
    total = refs[0][...]
    for ref in refs[1:-1]:
        total = total + ref[...].astype(F32)
    refs[-1][...] = total.astype(refs[-1].dtype)


def join(parts, dtype):
    return pl.pallas_call(
        join_kernel,
        in_specs=[pl.BlockSpec(memory_space=pltpu.VMEM)] * len(parts),
        out_specs=pl.BlockSpec(memory_space=pltpu.VMEM),
        out_shape=jax.ShapeDtypeStruct(parts[0].shape, dtype),
        compiler_params=params(True, 4),
        name="join_group",
    )(*parts)


def forward(core, grp, mine, theirs, cat, rel, block, flips):
    rows, depth = cat.shape
    width = mine.shape[1]
    args = (mine, theirs, cat, rel)
    outs = share_shapes(rows, width, flips)
    return pl.pallas_call(
        functools.partial(forward_kernel, block),
        grid_spec=pltpu.PrefetchScalarGridSpec(
            num_scalar_prefetch=2,
            grid=(1,),
            in_specs=[fixed(x.shape) for x in args],
            out_specs=[fixed(x) for x, _ in outs],
            scratch_shapes=[pltpu.VMEM((depth, width), BF), pltpu.VMEM((rows, width), F32)],
        ),
        out_shape=shaped(*outs),
        compiler_params=params(mine.shape[0] <= 512, 16),
        name="forward_partial",
    )(core, grp, *args)


def activate_kernel(planes, flips, cut, plane, grp, win_ref, wself_ref, *refs):
    agg_pieces = refs[: planes * flips]
    sources = refs[planes * flips : planes * flips + 6]
    outs = refs[planes * flips + 6 : planes * flips + 10]
    own_ref, *held, sems = refs[planes * flips + 10 :]
    agg_ref, node_ref, h_ref, d_ref = held
    rows = sources[0].shape[0]
    block = rows // flips
    for s in range(planes):
        j = lax.rem(plane[0] - s + planes, planes)
        for a in range(flips):
            at = rows_at(j * flips + (grp[0] ^ a), block)
            agg_ref[at, :] = agg_pieces[s * flips + a][...]
            if s > 0:
                which, row = stacked(s, a, cut, block)
                node_ref[at, :] = sources[which][row : row + block, :]
        if s == 0:
            node_ref[rows_at(j, rows), :] = sources[0][...]

    def embed(j, carry):
        at = rows_at(j, rows)
        act = jnp.tanh(dot(agg_ref[at, :], win_ref[...]) + dot(node_ref[at, :], wself_ref[...]))
        h_ref[at, :] = act.astype(BF)
        d_ref[at, :] = (1.0 - act * act).astype(BF)
        for n in range(4):
            pltpu.make_async_copy(held[n].at[at, :], outs[n].at[at, :], sems.at[n, j]).start()
        return carry

    def finish(j, carry):
        at = rows_at(j, rows)
        for n in range(4):
            pltpu.make_async_copy(held[n].at[at, :], outs[n].at[at, :], sems.at[n, j]).wait()
        return carry

    lax.fori_loop(0, planes, embed, 0)
    own_ref[...] = h_ref[rows_at(plane[0] * flips + grp[0], block), :]
    lax.fori_loop(0, planes, finish, 0)


def activate(plane, grp, agg_pieces, sources, w_in, w_self):
    rows, width = sources[0].shape
    block = agg_pieces[0].shape[0]
    flips = rows // block
    cut = 1 + sources[4].shape[0] // block
    planes = len(agg_pieces) // flips
    out = ((planes * rows, width), BF)
    args = (w_in, w_self, *agg_pieces, *sources)
    return pl.pallas_call(
        functools.partial(activate_kernel, planes, flips, cut),
        grid_spec=pltpu.PrefetchScalarGridSpec(
            num_scalar_prefetch=2,
            grid=(1,),
            in_specs=[fixed(x.shape) for x in args],
            out_specs=[pl.BlockSpec(memory_space=pl.ANY)] * 4 + [fixed((block, width))],
            scratch_shapes=[pltpu.VMEM(*out)] * 4 + [pltpu.SemaphoreType.DMA((4, planes))],
        ),
        out_shape=shaped(*[out] * 4, ((block, width), BF)),
        compiler_params=params(planes <= 4, 60),
        name="activate",
    )(plane, grp, *args)


def row_gradient(gs, h, start, qb_ref, qg_ref, meta_ref):
    step, width = h.shape
    count = qb_ref.shape[0]
    colsum = dot(gs, jnp.ones((count, 128), BF))
    colsum = jnp.concatenate([colsum] * (width // 128), axis=1)
    row = lax.broadcasted_iota(I32, (step, count), 0)
    picked = jnp.where(row == meta_ref[8:9, :] - start, 1.0, 0.0).astype(BF)
    grad = dot(gs, qb_ref[...]) - h.astype(F32) * colsum
    return 2.0 * width ** (-0.5) * grad + dot(picked, qg_ref[...])


def score_kernel(block, step, total_q, own_ref, other_ref, rel_ref, bias_ref, meta_ref, *refs):
    gs_ref, qg_ref, qb_ref, loss_ref = refs[:4]
    s_ref, ht_ref = refs[-2:]
    half, width = own_ref.shape
    qt = rel_ref.shape[0]
    scale = width ** (-0.5)
    blocks = step // block
    halves = ((0, own_ref), (half, other_ref))
    tail = meta_ref[0:1, :]
    head = jnp.broadcast_to(meta_ref[8:9, :].astype(F32), (128, qt)).T
    head = jnp.concatenate([head] * (step // 128), axis=1).astype(I32)

    q = rel_ref[...]
    for base, ref in halves:

        def pick(b, q):
            column = lax.broadcasted_iota(I32, (qt, step), 1)
            picked = jnp.where(column == head - (base + b * step), 1.0, 0.0).astype(BF)
            return q + dot(picked, ref[rows_at(b, step), :])

        q = lax.fori_loop(0, half // step, pick, q, unroll=4)
    qb_ref[...] = q.astype(BF)
    flipped = q.T
    hi, lo = split(flipped * (2.0 * scale))
    qsq = scale * jnp.sum(flipped * flipped, axis=0, keepdims=True)

    top = jnp.full((8, qt), 2.0 * NEG_FILL, F32)
    for base, ref in halves:

        def first(b, top):
            hb = ref[rows_at(b, step), :]
            cross = dot(hb, hi) + dot(hb, lo)
            x = hb.astype(F32)
            hsq = scale * jnp.sum(x * x, axis=1, keepdims=True)
            ht_ref[:, pl.ds(pl.multiple_of(base + b * step, step), step)] = hb.T
            for u in range(blocks):
                at = slice(u * block, (u + 1) * block)
                bias = bias_ref[pl.ds(base // block + b * blocks + u, 1), :] - qsq
                s = cross[at] - hsq[at] + bias
                s_ref[pl.ds(pl.multiple_of(base + b * step + u * block, block), block), :] = s
                top = jnp.maximum(top, jnp.max(s.reshape(block // 8, 8, qt), axis=0))
            return top

        top = lax.fori_loop(0, half // step, first, top, unroll=2)
    top = jnp.max(top, axis=0, keepdims=True)
    row = lax.broadcasted_iota(I32, (block, qt), 0)

    def second(b, carry):
        norm, truth = carry
        s = s_ref[rows_at(b, block), :]
        e = jnp.exp(s - top)
        s_ref[rows_at(b, block), :] = e
        at_tail = jnp.where(row == tail - b * block, s, 0.0)
        norm = norm + jnp.sum(e.reshape(block // 8, 8, qt), axis=0)
        truth = truth + jnp.sum(at_tail.reshape(block // 8, 8, qt), axis=0)
        return norm, truth

    zero = jnp.zeros((8, qt), F32)
    norm, truth = lax.fori_loop(0, 2 * half // block, second, (zero, zero))
    norm = jnp.sum(norm, axis=0, keepdims=True)
    truth = jnp.sum(truth, axis=0, keepdims=True)
    loss_ref[...] = top + jnp.log(norm) - truth
    inverse = 1.0 / norm
    share = inverse * (1.0 / total_q)

    def third(b, carry):
        picked = jnp.where(row == tail - b * block, 1.0 / total_q, 0.0)
        gs_ref[rows_at(b, block), :] = (s_ref[rows_at(b, block), :] * share - picked).astype(BF)
        return carry

    lax.fori_loop(0, 2 * half // block, third, 0)
    pulled = dot(ht_ref[...], gs_ref[...])
    rowsum = (norm * inverse - 1.0) * (1.0 / total_q)
    qg_ref[...] = (2.0 * scale * (pulled - flipped * rowsum)).T.astype(BF)
    for grad_ref in refs[4:-2]:

        def push(b, carry):
            at = pl.ds(pl.multiple_of(half + b * step, step), step)
            grad = row_gradient(
                gs_ref[at, :], other_ref[rows_at(b, step), :], half + b * step, qb_ref, qg_ref, meta_ref
            )
            grad_ref[rows_at(b, step), :] = grad.astype(BF)
            return carry

        lax.fori_loop(0, half // step, push, 0, unroll=2)


def score(own, other, rel, bias, meta, block, total_q):
    half, width = own.shape
    total = 2 * half
    count = rel.shape[0]
    whole = total * count <= 4096 * 512
    qt = count if whole else 128
    once = dict(pipeline_mode=pl.Buffered(1)) if whole else {}
    wide = pl.BlockSpec((qt, width), lambda i: (i, 0), **once)
    return pl.pallas_call(
        functools.partial(score_kernel, block, min(512, half), total_q),
        grid=(count // qt,),
        in_specs=[
            fixed(own.shape),
            fixed(other.shape),
            wide,
            pl.BlockSpec((bias.shape[0], qt), lambda i: (0, i), **once),
            pl.BlockSpec((meta.shape[0], qt), lambda i: (0, i), **once),
        ],
        out_specs=[
            pl.BlockSpec((total, qt), lambda i: (0, i), **once),
            wide,
            wide,
            pl.BlockSpec((1, qt), lambda i: (0, i), **once),
        ]
        + [fixed(other.shape)] * whole,
        out_shape=shaped(
            ((total, count), BF),
            ((count, width), BF),
            ((count, width), BF),
            ((1, count), F32),
            *[(other.shape, BF)] * whole,
        ),
        scratch_shapes=[pltpu.VMEM((total, qt), F32), pltpu.VMEM((width, total), BF)],
        compiler_params=params(whole, 28),
        cost_estimate=cost(60),
        name="score",
    )(own, other, rel, bias, meta)


def rows_kernel(base, gs_ref, qb_ref, qg_ref, meta_ref, h_ref, out_ref):
    start = base + pl.program_id(0) * h_ref.shape[0]
    grad = row_gradient(gs_ref[...], h_ref[...], start, qb_ref, qg_ref, meta_ref)
    out_ref[...] = grad.astype(BF)


def rows(base, gs, qb, qg, meta, h, name):
    half, width = h.shape
    count = qb.shape[0]
    step = min(512, half)
    tall = pl.BlockSpec((step, width), lambda i: (i, 0))
    return pl.pallas_call(
        functools.partial(rows_kernel, base),
        grid=(half // step,),
        in_specs=[
            pl.BlockSpec((step, count), lambda i: (i + base // step, 0)),
            fixed(qb.shape),
            fixed(qg.shape),
            fixed(meta.shape),
            tall,
        ],
        out_specs=tall,
        out_shape=jax.ShapeDtypeStruct((half, width), BF),
        compiler_params=params(half <= 2048, 10),
        cost_estimate=cost(0),
        name=name,
    )(gs, qb, qg, meta, h)


def backward_kernel(tiles, block, planes, plane, grp, own_ref, other_ref, d_ref, *refs):
    win_ref, wself_ref, send_ref, *refs = refs
    got = refs[: planes - 1]
    pre_ref, agg_grad_ref, mine_ref, theirs_ref, self_ref, owned, box, sems = refs[planes - 1 :]
    j = pl.program_id(0)
    used = 2 * block + INFO_ROWS

    @pl.when(j == 0)
    def _():
        owned[...] = jnp.zeros_like(owned)
        for s in range(planes):
            at = lax.rem(plane[0] - s + planes, planes)
            source = send_ref.at[plane[0]] if s == 0 else got[s - 1]
            pltpu.make_async_copy(source.at[0:used, :], box.at[at], sems.at[at]).start()

    pltpu.make_async_copy(send_ref.at[0, 0:used, :], box.at[j], sems.at[j]).wait()
    grad = own_ref[...].astype(F32) + other_ref[...].astype(F32)
    pre = (grad * d_ref[...].astype(F32)).astype(BF)
    pre_ref[...] = pre

    @pl.when(j == plane[0])
    def _():
        self_ref[...] = dot_nt(pre_ref[rows_at(grp[0], block), :], wself_ref[...])

    agg_grad = dot_nt(pre, win_ref[...]).astype(BF)
    agg_grad_ref[...] = agg_grad
    back = dot(box[j, 0 : 2 * block, :], agg_grad)
    info = box[j, 2 * block :, :].astype(F32)
    for s in range(2):
        part = back[s * block : (s + 1) * block]
        which = info[2 + s : 3 + s, 0:1]
        for t in range(tiles):
            owned[s * tiles + t] = owned[s * tiles + t] + jnp.where(which == t, part, 0.0)

    @pl.when(j == pl.num_programs(0) - 1)
    def _():
        for t in range(tiles):
            mine_ref[t * block : (t + 1) * block, :] = owned[t]
            theirs_ref[t * block : (t + 1) * block, :] = owned[tiles + t].astype(BF)


def backward(plane, grp, own, other, d, w_in, w_self, send, got, tiles, block):
    half, width = own.shape
    planes, _, node_rows = send.shape
    tall = pl.BlockSpec((node_rows, width), lambda i, *a: (i, 0))
    anywhere = pl.BlockSpec(memory_space=pl.ANY)
    return pl.pallas_call(
        functools.partial(backward_kernel, tiles, block, planes),
        grid_spec=pltpu.PrefetchScalarGridSpec(
            num_scalar_prefetch=2,
            grid=(planes,),
            in_specs=[tall] * 3 + [fixed(w_in.shape)] * 2 + [anywhere] * planes,
            out_specs=[tall, tall] + [fixed((node_rows, width))] * 2 + [fixed((block, width))],
            scratch_shapes=[
                pltpu.VMEM((2 * tiles, block, width), F32),
                pltpu.VMEM((planes, 2 * block + INFO_ROWS, node_rows), BF),
                pltpu.SemaphoreType.DMA((planes,)),
            ],
        ),
        out_shape=shaped(
            ((half, width), BF),
            ((half, width), BF),
            ((node_rows, width), F32),
            ((node_rows, width), BF),
            ((block, width), F32),
        ),
        compiler_params=params(planes <= 4, 16),
        cost_estimate=cost(6),
        name="backward_rows",
    )(plane, grp, own, other, d, w_in, w_self, send, *got)


def sums_kernel(skip, planes, plane, grp, core, pre_ref, agg_ref, node_ref, agg_grad_ref, *refs):
    mine_ref, theirs_ref, loss_ref, other_loss_ref, send_ref = refs[:5]
    got = refs[5 : planes + 4]
    out_ref, all_loss_ref, *share_refs = refs[planes + 4 : -5]
    total, gw, grel, box, sems = refs[-5:]
    j = pl.program_id(0)
    node_rows, width = pre_ref.shape
    used = box.shape[1]

    @pl.when(j == 0)
    def _():
        total[...] = mine_ref[...] + theirs_ref[...].astype(F32)
        put_shares(total, grp[0], share_refs)
        own, other = loss_ref[...], other_loss_ref[...]
        here = jnp.zeros(own.shape, I32) + core[0]
        all_loss_ref[0:1, :] = jnp.where(here == 0, own, other)
        all_loss_ref[1:2, :] = jnp.where(here == 0, other, own)
        gw[...] = jnp.zeros_like(gw)
        grel[...] = jnp.zeros_like(grel)
        for s in range(planes):
            at = lax.rem(plane[0] - s + planes, planes)
            source = send_ref.at[plane[0]] if s == 0 else got[s - 1]
            pltpu.make_async_copy(source.at[skip : skip + used, :], box.at[at], sems.at[at]).start()

    pltpu.make_async_copy(send_ref.at[0, skip : skip + used, :], box.at[j], sems.at[j]).wait()
    quarter = used - INFO_ROWS
    tiles = node_rows // 128
    count = tiles * quarter
    cut = [slice(t * 128, (t + 1) * 128) for t in range(tiles)]
    line = jnp.concatenate([box[j, INFO_ROWS:, at] for at in cut], axis=0).astype(F32)
    info = box[j, 0:INFO_ROWS, :].astype(F32)
    target = jnp.broadcast_to(info[1:2, 0:count], (128, count)).T[:, 0:1]
    spread = [jnp.where(target == t, line, 0.0) for t in range(tiles)]
    hi, lo = split(dot(jnp.concatenate(spread, axis=1).astype(BF), agg_grad_ref[...]))
    relation = lax.broadcasted_iota(I32, (grel.shape[0], count), 0).astype(F32)
    chosen = jnp.where(relation == info[0:1, 0:count], 1.0, 0.0).astype(BF)
    grel[...] = grel[...] - (dot(chosen, hi) + dot(chosen, lo))
    flipped = pre_ref[...].astype(F32).T.astype(BF)
    gw[0] = gw[0] + dot(flipped, agg_ref[...])
    gw[1] = gw[1] + dot(flipped, node_ref[...])

    @pl.when(j == pl.num_programs(0) - 1)
    def _():
        out_ref[0:width, :] = gw[0].T.astype(BF)
        out_ref[width : 2 * width, :] = gw[1].T.astype(BF)
        out_ref[2 * width :, :] = grel[...].astype(BF)


def sums_of_half(
    places, pre, agg, nodes, agg_grad, mine, theirs, loss, other_loss, send, got, skip, rel_rows, flips
):
    width = pre.shape[1]
    small = (mine, theirs, loss, other_loss)
    planes, send_rows, node_rows = send.shape
    tall = pl.BlockSpec((node_rows, width), lambda i, *a: (i, 0))
    anywhere = pl.BlockSpec(memory_space=pl.ANY)
    outs = [
        ((2 * width + rel_rows, width), BF),
        ((2, loss.shape[1]), F32),
        *share_shapes(*mine.shape, flips),
    ]
    return pl.pallas_call(
        functools.partial(sums_kernel, skip, planes),
        grid_spec=pltpu.PrefetchScalarGridSpec(
            num_scalar_prefetch=3,
            grid=(planes,),
            in_specs=[tall] * 4 + [fixed(x.shape) for x in small] + [anywhere] * planes,
            out_specs=[fixed(x) for x, _ in outs],
            scratch_shapes=[
                pltpu.VMEM(mine.shape, F32),
                pltpu.VMEM((2, width, width), F32),
                pltpu.VMEM((rel_rows, width), F32),
                pltpu.VMEM((planes, send_rows - skip, node_rows), BF),
                pltpu.SemaphoreType.DMA((planes,)),
            ],
        ),
        out_shape=shaped(*outs),
        compiler_params=params(planes <= 4, 20),
        cost_estimate=cost(20),
        name="sums_of_half",
    )(*places, pre, agg, nodes, agg_grad, *small, send, *got)


def shift_planes(x, by, cand_count):
    return lax.ppermute(x, "cand", [(i, (i + 2 * by) % cand_count) for i in range(cand_count)])


def swap_core(x, cand_count):
    return lax.ppermute(x, "cand", [(i, i ^ 1) for i in range(cand_count)])


def swap_grp(x, flip, grp_count):
    return lax.ppermute(x, "grp", [(i, i ^ flip) for i in range(grp_count)])


def total_kernel(a_ref, b_ref, gwin_ref, gwself_ref, grel_ref):
    start = 0
    for ref in (gwin_ref, gwself_ref, grel_ref):
        at = slice(start, start + ref.shape[0])
        ref[...] = a_ref[at, :].astype(F32) + b_ref[at, :].astype(F32)
        start += ref.shape[0]


def total_sums(a, b, rel_count):
    width = a.shape[1]
    outs = [((n, width), F32) for n in (width, width, rel_count)]
    return pl.pallas_call(
        total_kernel,
        in_specs=[pl.BlockSpec(memory_space=pltpu.VMEM)] * 2,
        out_specs=[pl.BlockSpec(memory_space=pltpu.VMEM)] * 3,
        out_shape=shaped(*outs),
        compiler_params=params(True, 12),
        name="total_sums",
    )(a, b)


def gather_planes(x, cand_count):
    return [x] + [shift_planes(x, s, cand_count) for s in range(1, cand_count // 2)]


def gather_stacks(here, block, grp_count):
    one, two = swap_grp(here, 1, grp_count), swap_grp(here, 2, grp_count)
    cut = here.shape[0] // block // 2 * block
    return [
        here,
        one,
        two,
        swap_grp(one[:cut], 2, grp_count),
        swap_grp(two[cut:], 1, grp_count),
    ]


def gather_pieces(planes, first, cand_count, grp_count):
    pieces = []
    for s in range(first, cand_count // 2):
        found = [planes[s]]
        for flip in range(1, grp_count):
            low, high = flip & -flip, flip - (flip & -flip)
            if high == 0:
                found.append(swap_grp(planes[s], flip, grp_count))
            elif s % 2:
                found.append(swap_grp(found[low], high, grp_count))
            else:
                found.append(swap_grp(found[high], low, grp_count))
        pieces += found
    return pieces


def swap_shares(parts, grp_count):
    return [swap_grp(part, flip + 1, grp_count) for flip, part in enumerate(parts)]


def body(
    node_emb,
    rel_emb,
    w_in,
    w_self,
    rel_score,
    mirror_blocks,
    adj_values,
    adj_source,
    adj_target,
    adj_relation,
    live_blocks,
    query_head,
    query_rel,
    allowed,
    true_tail,
):
    cand_count = lax.axis_size("cand")
    grp_count = lax.axis_size("grp")
    grp_index = lax.axis_index("grp").astype(I32)
    cand_index = lax.axis_index("cand").astype(I32)
    nodes = node_emb[0]
    node_rows, width = nodes.shape
    block = adj_values.shape[-1]
    tiles = node_rows // block
    share_rows = node_rows // grp_count
    plane_count = cand_count // 2
    plane, core = cand_index // 2, cand_index % 2
    half = plane_count * node_rows
    want = mirror_blocks.reshape(-1)
    total_q = query_head.shape[0]
    half_q = total_q // 2
    rel_rows = -(-rel_emb.shape[0] // 128) * 128

    own_share = lax.dynamic_slice_in_dim(nodes, grp_index * share_rows, share_rows, 0)
    their_want = swap_core(want, cand_count)
    stack = jnp.concatenate(gather_planes(own_share, cand_count)[1:])
    cat, send = fold(
        adj_values[0, 0],
        adj_source[0, 0],
        adj_target[0, 0],
        adj_relation[0, 0],
        live_blocks[0],
        want,
        core[None],
        tiles,
        rel_rows,
    )
    stack, cat, send = lax.optimization_barrier((stack, cat, send))
    nodes_at = [nodes, *gather_stacks(stack, share_rows, grp_count)]

    def own_half(x):
        return lax.dynamic_slice_in_dim(x, core * half_q, half_q, 0)

    def order(ids):
        cand = ids // node_rows
        return ((cand % 2) ^ core) * half + (cand // 2) * node_rows + ids % node_rows

    rel_q = jnp.take(rel_score, own_half(query_rel), axis=0)
    allowed_at = order(own_half(allowed) * block) // block
    block_ids = jnp.arange(2 * half // block, dtype=I32)
    hit = jnp.any(allowed_at.T[:, None, :] == block_ids[None, :, None], axis=0)
    bias = jnp.where(hit, 0.0, NEG_FILL).astype(F32)
    meta = jnp.concatenate(
        [
            jnp.broadcast_to(order(own_half(true_tail))[None], (8, half_q)),
            jnp.broadcast_to(order(own_half(query_head))[None], (8, half_q)),
        ]
    )
    *nodes_at, rel_q, bias, meta = lax.optimization_barrier((*nodes_at, rel_q, bias, meta))
    mine, theirs = pick(
        plane[None], grp_index[None], core[None], want, their_want, nodes_at, block
    )
    theirs = swap_core(theirs, cand_count)
    own, *parts = forward(
        core[None], grp_index[None], mine, theirs, cat, rel_emb, block, grp_count
    )
    own_agg = join([own, *swap_shares(parts, grp_count)], BF)
    agg_planes = gather_planes(own_agg, cand_count)
    agg_pieces = gather_pieces(agg_planes, 0, cand_count, grp_count)

    agg_pieces, rel_q, bias, meta = lax.optimization_barrier((agg_pieces, rel_q, bias, meta))
    half_agg, half_nodes, half_h, half_d, h_own = activate(
        plane[None], grp_index[None], agg_pieces, nodes_at, w_in, w_self
    )

    other_h = swap_core(half_h, cand_count)

    def send_to_plane(x, by):
        part = lax.dynamic_index_in_dim(x, (plane + by) % plane_count, 0, keepdims=False)
        return shift_planes(part, by, cand_count)

    send_after = lax.optimization_barrier((send, half_h))[0]
    got = [send_to_plane(send_after, by) for by in range(1, plane_count)]
    gs, qg, qb, loss, *out_grad = score(half_h, other_h, rel_q, bias, meta, block, total_q)
    gs, *more = lax.optimization_barrier((gs, *out_grad, *got))
    out_grad, got = more[: len(out_grad)], more[len(out_grad) :]
    other_loss = swap_core(loss, cand_count)
    out_grad = out_grad[0] if out_grad else rows(half, gs, qb, qg, meta, other_h, "rows_other")
    in_grad = swap_core(out_grad, cand_count)
    own_grad = rows(0, gs, qb, qg, meta, half_h, "rows_own")
    pre, agg_grad, mine, theirs, self_grad = backward(
        plane[None],
        grp_index[None],
        own_grad,
        in_grad,
        half_d,
        w_in,
        w_self,
        send,
        got,
        tiles,
        block,
    )
    sums, loss, own, *parts = sums_of_half(
        (plane[None], grp_index[None], core[None]),
        pre,
        half_agg,
        half_nodes,
        agg_grad,
        mine,
        swap_core(theirs, cand_count),
        loss,
        other_loss,
        send,
        got,
        2 * block,
        rel_rows,
        grp_count,
    )
    gwin, gwself, grel = total_sums(sums, swap_core(sums, cand_count), rel_emb.shape[0])
    own, gwin, gwself, grel = lax.optimization_barrier((own, gwin, gwself, grel))
    node_grad = join([own, self_grad, *swap_shares(parts, grp_count)], F32)
    return (
        h_own[None],
        loss.reshape(total_q),
        node_grad[None],
        grel,
        gwin,
        gwself,
    )


def solution(mesh):
    return jax.shard_map(
        body,
        mesh=mesh,
        in_specs=(
            P("cand", None, None),
            P("grp", None),
            P(),
            P(),
            P(),
            P("grp", "cand", None, None),
            P("grp", "cand", None, None, None),
            P("grp", "cand", None),
            P("grp", "cand", None),
            P("grp", "cand", None),
            P("grp", "cand"),
            P(),
            P(),
            P(),
            P(),
        ),
        out_specs=(P("cand", "grp", None), P(), P("cand", "grp", None), P("grp", None), P(), P()),
        check_vma=False,
    )
```

```python
import functools

import jax
import jax.numpy as jnp
from jax import lax
from jax.experimental import pallas as pl
from jax.experimental.pallas import tpu as pltpu
from jax.sharding import PartitionSpec as P

NEG_FILL = -1e30
BF = jnp.bfloat16
F32 = jnp.float32
I32 = jnp.int32
INFO_ROWS = 16


def dot(a, b):
    return jnp.dot(a, b, preferred_element_type=F32)


def dot_nt(a, b):
    return lax.dot_general(a, b, (((1,), (1,)), ((), ())), preferred_element_type=F32)


def split(x):
    hi = x.astype(BF)
    return hi, (x - hi.astype(F32)).astype(BF)


def params(small, mebibytes):
    return pltpu.CompilerParams(vmem_limit_bytes=(mebibytes if small else 60) * 1024 * 1024)


def fixed(shape):
    return pl.BlockSpec(shape, lambda *a: (0,) * len(shape), pipeline_mode=pl.Buffered(1))


def shaped(*pairs):
    return [jax.ShapeDtypeStruct(s, d) for s, d in pairs]


def cost(micros):
    return pl.CostEstimate(flops=micros * 10**9, bytes_accessed=micros * 10**6, transcendentals=0)


def rows_at(index, size):
    return pl.ds(pl.multiple_of(index * size, size), size)


def fold_kernel(tiles, per, src, tgt, rel, live, want, core, a_ref, info_ref, *refs):
    cat_ref, send_ref, acc, wacc, line = refs
    step = pl.program_id(0)
    block = a_ref.shape[1]
    slots = want.shape[0]
    rel_rows = (wacc.shape[0] - 8) // tiles
    count = line.shape[0]

    @pl.when(step == 0)
    def _():
        acc[...] = jnp.zeros_like(acc)
        wacc[...] = jnp.zeros_like(wacc)

    sums = dot_nt(jnp.ones((8, block), BF), a_ref[...].reshape(per * block, block))
    for i in range(per):
        b = step * per + i
        good = b < live[0]
        at = jnp.where(good, tgt[b] * slots + src[b], tiles * slots)
        acc[at] = acc[at] + a_ref[i].astype(F32)
        row = jnp.where(good, tgt[b] * rel_rows + rel[b], tiles * rel_rows)
        total = sums[0:1, i * block : (i + 1) * block]
        wacc[pl.ds(row, 1), :] = wacc[pl.ds(row, 1), :] + total
        line[pl.ds(b, 1), :] = jnp.where(good, total, 0.0)

    @pl.when(step == pl.num_programs(0) - 1)
    def _():
        base = 2 * slots * block
        quarter = count // tiles
        tail = 2 * block + INFO_ROWS
        row = lax.broadcasted_iota(I32, info_ref.shape, 0)
        for z in range(slots // 2):
            info = info_ref[...]
            for n in range(2):
                info = jnp.where(row == 2 + n, want[2 * z + (n ^ core[0])].astype(F32), info)
            send_ref[z, 2 * block : tail, :] = info.astype(BF)
            for t in range(tiles):
                those = line[t * quarter : (t + 1) * quarter, :]
                send_ref[z, tail:, t * block : (t + 1) * block] = those.astype(BF)
        for t in range(tiles):
            at = slice(t * block, (t + 1) * block)
            hi, lo = split(-wacc[t * rel_rows : (t + 1) * rel_rows, :].T)
            cat_ref[at, base : base + rel_rows] = hi
            cat_ref[at, base + rel_rows : base + 2 * rel_rows] = hi
            cat_ref[at, base + 2 * rel_rows :] = lo
            for s in range(slots):
                part = acc[t * slots + s]
                hi, lo = split(part)
                cat_ref[at, s * block : (s + 1) * block] = hi
                cat_ref[at, (slots + s) * block : (slots + s + 1) * block] = lo
                send_ref[s // 2, rows_at(s % 2 ^ core[0], block), at] = part.T.astype(BF)


def fold(adj, src, tgt, rel, live, want, core, tiles, rel_rows):
    count, block, _ = adj.shape
    slots = want.shape[0]
    per = next(p for p in (96, 48, 16, 8, 4, 2, 1) if count % p == 0)
    rows = tiles * block
    info = jnp.pad(jnp.stack([rel, tgt]).astype(F32), ((0, INFO_ROWS - 2), (0, rows - count)))
    outs = [
        ((rows, 2 * slots * block + 3 * rel_rows), BF),
        ((slots // 2, 2 * block + INFO_ROWS + count // tiles, rows), BF),
    ]
    return pl.pallas_call(
        functools.partial(fold_kernel, tiles, per),
        grid_spec=pltpu.PrefetchScalarGridSpec(
            num_scalar_prefetch=6,
            grid=(count // per,),
            in_specs=[
                pl.BlockSpec((per, block, block), lambda i, *a: (i, 0, 0)),
                fixed((INFO_ROWS, rows)),
            ],
            out_specs=[fixed(s) for s, _ in outs],
            scratch_shapes=[
                pltpu.VMEM((tiles * slots + 1, block, block), F32),
                pltpu.VMEM((tiles * rel_rows + 8, block), F32),
                pltpu.VMEM((count, block), F32),
            ],
        ),
        out_shape=shaped(*outs),
        compiler_params=params(slots <= 8, 60),
        cost_estimate=cost(8),
        name="fold_adjacency",
    )(src, tgt, rel, live, want, core, adj, info)


def stacked(shift, flip, cut, block):
    if shift == 0:
        return 0, None
    if flip < 3:
        return 1 + flip, (shift - 1) * block
    return (4, (shift - 1) * block) if shift < cut else (5, (shift - cut) * block)


def pick_kernel(planes, block, cut, plane, grp, core, mine, theirs, *refs):
    sources, (mine_ref, theirs_ref, sems) = refs[:-3], refs[-3:]
    flips = sources[0].shape[0] // block
    for wait in (False, True):
        for n, (ids, out_ref) in enumerate(((mine, mine_ref), (theirs, theirs_ref))):
            for s in range(planes):
                j = lax.rem(plane[0] - s + planes, planes)
                tile = ids[2 * j + core[0]]
                for a in range(1 if s == 0 or wait else flips):
                    which, row = stacked(s, a, cut, block)
                    if s == 0:
                        source = sources[0].at[rows_at(tile, block), :]
                    else:
                        source = sources[which].at[row : row + block, :]
                    target = out_ref.at[rows_at(j, block), :]
                    copy = pltpu.make_async_copy(source, target, sems.at[n, s])
                    if wait:
                        copy.wait()
                    elif s == 0:
                        copy.start()
                    else:

                        @pl.when((tile ^ grp[0]) == a)
                        def _():
                            copy.start()


def pick(plane, grp, core, mine, theirs, sources, block):
    planes = mine.shape[0] // 2
    out = ((planes * block, sources[0].shape[1]), BF)
    cut = 1 + sources[4].shape[0] // block
    anywhere = pl.BlockSpec(memory_space=pl.ANY)
    return pl.pallas_call(
        functools.partial(pick_kernel, planes, block, cut),
        grid_spec=pltpu.PrefetchScalarGridSpec(
            num_scalar_prefetch=5,
            grid=(1,),
            in_specs=[anywhere] * len(sources),
            out_specs=[fixed(out[0])] * 2,
            scratch_shapes=[pltpu.SemaphoreType.DMA((2, planes))],
        ),
        out_shape=shaped(out, out),
        compiler_params=params(planes <= 4, 6),
        name="pick_mirrors",
    )(plane, grp, core, mine, theirs, *sources)


def forward_kernel(block, core, grp, mine_ref, theirs_ref, cat_ref, rel_ref, *refs):
    *share_refs, right, total = refs
    depth = 2 * mine_ref.shape[0]
    rel_count = rel_ref.shape[0]
    rel_rows = (right.shape[0] - 2 * depth) // 3
    for j in range(mine_ref.shape[0] // block):
        at = slice(j * block, (j + 1) * block)
        for base in (0, depth // block):
            right[rows_at(base + 2 * j + core[0], block), :] = mine_ref[at, :]
            right[rows_at(base + 2 * j + 1 - core[0], block), :] = theirs_ref[at, :]
    hi, lo = split(rel_ref[...])
    for i, part in enumerate((hi, lo, hi)):
        base = 2 * depth + i * rel_rows
        edge = rel_count // 16 * 16
        right[base + edge : base + rel_rows, :] = jnp.zeros((rel_rows - edge, right.shape[1]), BF)
        right[base : base + rel_count, :] = part
    total[...] = dot(cat_ref[...], right[...])
    put_shares(total, grp[0], share_refs)


def put_shares(total, grp, refs):
    for flip, ref in enumerate(refs):
        ref[...] = total[rows_at(grp ^ flip, ref.shape[0]), :].astype(ref.dtype)


def share_shapes(rows, width, flips):
    return [((rows // flips, width), BF if flip else F32) for flip in range(flips)]


def join_kernel(*refs):
    total = refs[0][...]
    for ref in refs[1:-1]:
        total = total + ref[...].astype(F32)
    refs[-1][...] = total.astype(refs[-1].dtype)


def join(parts, dtype):
    return pl.pallas_call(
        join_kernel,
        in_specs=[pl.BlockSpec(memory_space=pltpu.VMEM)] * len(parts),
        out_specs=pl.BlockSpec(memory_space=pltpu.VMEM),
        out_shape=jax.ShapeDtypeStruct(parts[0].shape, dtype),
        compiler_params=params(True, 4),
        name="join_group",
    )(*parts)


def forward(core, grp, mine, theirs, cat, rel, block, flips):
    rows, depth = cat.shape
    width = mine.shape[1]
    args = (mine, theirs, cat, rel)
    outs = share_shapes(rows, width, flips)
    return pl.pallas_call(
        functools.partial(forward_kernel, block),
        grid_spec=pltpu.PrefetchScalarGridSpec(
            num_scalar_prefetch=2,
            grid=(1,),
            in_specs=[fixed(x.shape) for x in args],
            out_specs=[fixed(x) for x, _ in outs],
            scratch_shapes=[pltpu.VMEM((depth, width), BF), pltpu.VMEM((rows, width), F32)],
        ),
        out_shape=shaped(*outs),
        compiler_params=params(mine.shape[0] <= 512, 16),
        name="forward_partial",
    )(core, grp, *args)


def activate_kernel(planes, flips, cut, plane, grp, win_ref, wself_ref, *refs):
    agg_pieces = refs[: planes * flips]
    sources = refs[planes * flips : planes * flips + 6]
    outs = refs[planes * flips + 6 : planes * flips + 10]
    own_ref, *held, sems = refs[planes * flips + 10 :]
    agg_ref, node_ref, h_ref, d_ref = held
    rows = sources[0].shape[0]
    block = rows // flips
    for s in range(planes):
        j = lax.rem(plane[0] - s + planes, planes)
        for a in range(flips):
            at = rows_at(j * flips + (grp[0] ^ a), block)
            agg_ref[at, :] = agg_pieces[s * flips + a][...]
            if s > 0:
                which, row = stacked(s, a, cut, block)
                node_ref[at, :] = sources[which][row : row + block, :]
        if s == 0:
            node_ref[rows_at(j, rows), :] = sources[0][...]

    def embed(j, carry):
        at = rows_at(j, rows)
        act = jnp.tanh(dot(agg_ref[at, :], win_ref[...]) + dot(node_ref[at, :], wself_ref[...]))
        h_ref[at, :] = act.astype(BF)
        d_ref[at, :] = (1.0 - act * act).astype(BF)
        for n in range(4):
            pltpu.make_async_copy(held[n].at[at, :], outs[n].at[at, :], sems.at[n, j]).start()
        return carry

    def finish(j, carry):
        at = rows_at(j, rows)
        for n in range(4):
            pltpu.make_async_copy(held[n].at[at, :], outs[n].at[at, :], sems.at[n, j]).wait()
        return carry

    lax.fori_loop(0, planes, embed, 0)
    own_ref[...] = h_ref[rows_at(plane[0] * flips + grp[0], block), :]
    lax.fori_loop(0, planes, finish, 0)


def activate(plane, grp, agg_pieces, sources, w_in, w_self):
    rows, width = sources[0].shape
    block = agg_pieces[0].shape[0]
    flips = rows // block
    cut = 1 + sources[4].shape[0] // block
    planes = len(agg_pieces) // flips
    out = ((planes * rows, width), BF)
    args = (w_in, w_self, *agg_pieces, *sources)
    return pl.pallas_call(
        functools.partial(activate_kernel, planes, flips, cut),
        grid_spec=pltpu.PrefetchScalarGridSpec(
            num_scalar_prefetch=2,
            grid=(1,),
            in_specs=[fixed(x.shape) for x in args],
            out_specs=[pl.BlockSpec(memory_space=pl.ANY)] * 4 + [fixed((block, width))],
            scratch_shapes=[pltpu.VMEM(*out)] * 4 + [pltpu.SemaphoreType.DMA((4, planes))],
        ),
        out_shape=shaped(*[out] * 4, ((block, width), BF)),
        compiler_params=params(planes <= 4, 60),
        name="activate",
    )(plane, grp, *args)


def row_gradient(gs, h, start, qb_ref, qg_ref, meta_ref):
    step, width = h.shape
    count = qb_ref.shape[0]
    colsum = dot(gs, jnp.ones((count, 128), BF))
    colsum = jnp.concatenate([colsum] * (width // 128), axis=1)
    row = lax.broadcasted_iota(I32, (step, count), 0)
    picked = jnp.where(row == meta_ref[8:9, :] - start, 1.0, 0.0).astype(BF)
    grad = dot(gs, qb_ref[...]) - h.astype(F32) * colsum
    return 2.0 * width ** (-0.5) * grad + dot(picked, qg_ref[...])


def score_kernel(block, step, total_q, own_ref, other_ref, rel_ref, bias_ref, meta_ref, *refs):
    gs_ref, qg_ref, qb_ref, loss_ref = refs[:4]
    s_ref, ht_ref = refs[-2:]
    half, width = own_ref.shape
    qt = rel_ref.shape[0]
    scale = width ** (-0.5)
    blocks = step // block
    halves = ((0, own_ref), (half, other_ref))
    tail = meta_ref[0:1, :]
    head = jnp.broadcast_to(meta_ref[8:9, :].astype(F32), (128, qt)).T
    head = jnp.concatenate([head] * (step // 128), axis=1).astype(I32)

    q = rel_ref[...]
    for base, ref in halves:

        def pick(b, q):
            column = lax.broadcasted_iota(I32, (qt, step), 1)
            picked = jnp.where(column == head - (base + b * step), 1.0, 0.0).astype(BF)
            return q + dot(picked, ref[rows_at(b, step), :])

        q = lax.fori_loop(0, half // step, pick, q, unroll=4)
    qb_ref[...] = q.astype(BF)
    flipped = q.T
    hi, lo = split(flipped * (2.0 * scale))
    qsq = scale * jnp.sum(flipped * flipped, axis=0, keepdims=True)

    top = jnp.full((8, qt), 2.0 * NEG_FILL, F32)
    for base, ref in halves:

        def first(b, top):
            hb = ref[rows_at(b, step), :]
            cross = dot(hb, hi) + dot(hb, lo)
            x = hb.astype(F32)
            hsq = scale * jnp.sum(x * x, axis=1, keepdims=True)
            ht_ref[:, pl.ds(pl.multiple_of(base + b * step, step), step)] = hb.T
            for u in range(blocks):
                at = slice(u * block, (u + 1) * block)
                bias = bias_ref[pl.ds(base // block + b * blocks + u, 1), :] - qsq
                s = cross[at] - hsq[at] + bias
                s_ref[pl.ds(pl.multiple_of(base + b * step + u * block, block), block), :] = s
                top = jnp.maximum(top, jnp.max(s.reshape(block // 8, 8, qt), axis=0))
            return top

        top = lax.fori_loop(0, half // step, first, top, unroll=2)
    top = jnp.max(top, axis=0, keepdims=True)
    row = lax.broadcasted_iota(I32, (block, qt), 0)

    def second(b, carry):
        norm, truth = carry
        s = s_ref[rows_at(b, block), :]
        e = jnp.exp(s - top)
        s_ref[rows_at(b, block), :] = e
        at_tail = jnp.where(row == tail - b * block, s, 0.0)
        norm = norm + jnp.sum(e.reshape(block // 8, 8, qt), axis=0)
        truth = truth + jnp.sum(at_tail.reshape(block // 8, 8, qt), axis=0)
        return norm, truth

    zero = jnp.zeros((8, qt), F32)
    norm, truth = lax.fori_loop(0, 2 * half // block, second, (zero, zero))
    norm = jnp.sum(norm, axis=0, keepdims=True)
    truth = jnp.sum(truth, axis=0, keepdims=True)
    loss_ref[...] = top + jnp.log(norm) - truth
    inverse = 1.0 / norm
    share = inverse * (1.0 / total_q)

    def third(b, carry):
        picked = jnp.where(row == tail - b * block, 1.0 / total_q, 0.0)
        gs_ref[rows_at(b, block), :] = (s_ref[rows_at(b, block), :] * share - picked).astype(BF)
        return carry

    lax.fori_loop(0, 2 * half // block, third, 0)
    pulled = dot(ht_ref[...], gs_ref[...])
    rowsum = (norm * inverse - 1.0) * (1.0 / total_q)
    qg_ref[...] = (2.0 * scale * (pulled - flipped * rowsum)).T.astype(BF)
    for grad_ref in refs[4:-2]:

        def push(b, carry):
            at = pl.ds(pl.multiple_of(half + b * step, step), step)
            grad = row_gradient(
                gs_ref[at, :], other_ref[rows_at(b, step), :], half + b * step, qb_ref, qg_ref, meta_ref
            )
            grad_ref[rows_at(b, step), :] = grad.astype(BF)
            return carry

        lax.fori_loop(0, half // step, push, 0, unroll=2)


def score(own, other, rel, bias, meta, block, total_q):
    half, width = own.shape
    total = 2 * half
    count = rel.shape[0]
    whole = total * count <= 4096 * 512
    qt = count if whole else 128
    once = dict(pipeline_mode=pl.Buffered(1)) if whole else {}
    wide = pl.BlockSpec((qt, width), lambda i: (i, 0), **once)
    return pl.pallas_call(
        functools.partial(score_kernel, block, min(512, half), total_q),
        grid=(count // qt,),
        in_specs=[
            fixed(own.shape),
            fixed(other.shape),
            wide,
            pl.BlockSpec((bias.shape[0], qt), lambda i: (0, i), **once),
            pl.BlockSpec((meta.shape[0], qt), lambda i: (0, i), **once),
        ],
        out_specs=[
            pl.BlockSpec((total, qt), lambda i: (0, i), **once),
            wide,
            wide,
            pl.BlockSpec((1, qt), lambda i: (0, i), **once),
        ]
        + [fixed(other.shape)] * whole,
        out_shape=shaped(
            ((total, count), BF),
            ((count, width), BF),
            ((count, width), BF),
            ((1, count), F32),
            *[(other.shape, BF)] * whole,
        ),
        scratch_shapes=[pltpu.VMEM((total, qt), F32), pltpu.VMEM((width, total), BF)],
        compiler_params=params(whole, 36),
        cost_estimate=cost(60),
        name="score",
    )(own, other, rel, bias, meta)


def rows_kernel(base, gs_ref, qb_ref, qg_ref, meta_ref, h_ref, out_ref):
    start = base + pl.program_id(0) * h_ref.shape[0]
    grad = row_gradient(gs_ref[...], h_ref[...], start, qb_ref, qg_ref, meta_ref)
    out_ref[...] = grad.astype(BF)


def rows(base, gs, qb, qg, meta, h, name):
    half, width = h.shape
    count = qb.shape[0]
    step = min(512, half)
    tall = pl.BlockSpec((step, width), lambda i: (i, 0))
    return pl.pallas_call(
        functools.partial(rows_kernel, base),
        grid=(half // step,),
        in_specs=[
            pl.BlockSpec((step, count), lambda i: (i + base // step, 0)),
            fixed(qb.shape),
            fixed(qg.shape),
            fixed(meta.shape),
            tall,
        ],
        out_specs=tall,
        out_shape=jax.ShapeDtypeStruct((half, width), BF),
        compiler_params=params(half <= 2048, 10),
        cost_estimate=cost(0),
        name=name,
    )(gs, qb, qg, meta, h)


def backward_kernel(tiles, block, planes, plane, grp, own_ref, other_ref, d_ref, *refs):
    win_ref, wself_ref, send_ref, *refs = refs
    got = refs[: planes - 1]
    pre_ref, agg_grad_ref, mine_ref, theirs_ref, self_ref, owned, box, sems = refs[planes - 1 :]
    j = pl.program_id(0)
    used = 2 * block + INFO_ROWS

    @pl.when(j == 0)
    def _():
        owned[...] = jnp.zeros_like(owned)
        for s in range(planes):
            at = lax.rem(plane[0] - s + planes, planes)
            source = send_ref.at[plane[0]] if s == 0 else got[s - 1]
            pltpu.make_async_copy(source.at[0:used, :], box.at[at], sems.at[at]).start()

    pltpu.make_async_copy(send_ref.at[0, 0:used, :], box.at[j], sems.at[j]).wait()
    grad = own_ref[...].astype(F32) + other_ref[...].astype(F32)
    pre = (grad * d_ref[...].astype(F32)).astype(BF)
    pre_ref[...] = pre

    @pl.when(j == plane[0])
    def _():
        self_ref[...] = dot_nt(pre_ref[rows_at(grp[0], block), :], wself_ref[...])

    agg_grad = dot_nt(pre, win_ref[...]).astype(BF)
    agg_grad_ref[...] = agg_grad
    back = dot(box[j, 0 : 2 * block, :], agg_grad)
    info = box[j, 2 * block :, :].astype(F32)
    for s in range(2):
        part = back[s * block : (s + 1) * block]
        which = info[2 + s : 3 + s, 0:1]
        for t in range(tiles):
            owned[s * tiles + t] = owned[s * tiles + t] + jnp.where(which == t, part, 0.0)

    @pl.when(j == pl.num_programs(0) - 1)
    def _():
        for t in range(tiles):
            mine_ref[t * block : (t + 1) * block, :] = owned[t]
            theirs_ref[t * block : (t + 1) * block, :] = owned[tiles + t].astype(BF)


def backward(plane, grp, own, other, d, w_in, w_self, send, got, tiles, block):
    half, width = own.shape
    planes, _, node_rows = send.shape
    tall = pl.BlockSpec((node_rows, width), lambda i, *a: (i, 0))
    anywhere = pl.BlockSpec(memory_space=pl.ANY)
    return pl.pallas_call(
        functools.partial(backward_kernel, tiles, block, planes),
        grid_spec=pltpu.PrefetchScalarGridSpec(
            num_scalar_prefetch=2,
            grid=(planes,),
            in_specs=[tall] * 3 + [fixed(w_in.shape)] * 2 + [anywhere] * planes,
            out_specs=[tall, tall] + [fixed((node_rows, width))] * 2 + [fixed((block, width))],
            scratch_shapes=[
                pltpu.VMEM((2 * tiles, block, width), F32),
                pltpu.VMEM((planes, 2 * block + INFO_ROWS, node_rows), BF),
                pltpu.SemaphoreType.DMA((planes,)),
            ],
        ),
        out_shape=shaped(
            ((half, width), BF),
            ((half, width), BF),
            ((node_rows, width), F32),
            ((node_rows, width), BF),
            ((block, width), F32),
        ),
        compiler_params=params(planes <= 4, 16),
        cost_estimate=cost(6),
        name="backward_rows",
    )(plane, grp, own, other, d, w_in, w_self, send, *got)


def sums_kernel(skip, planes, plane, grp, core, pre_ref, agg_ref, node_ref, agg_grad_ref, *refs):
    mine_ref, theirs_ref, loss_ref, other_loss_ref, send_ref = refs[:5]
    got = refs[5 : planes + 4]
    out_ref, all_loss_ref, *share_refs = refs[planes + 4 : -5]
    total, gw, grel, box, sems = refs[-5:]
    j = pl.program_id(0)
    node_rows, width = pre_ref.shape
    used = box.shape[1]

    @pl.when(j == 0)
    def _():
        total[...] = mine_ref[...] + theirs_ref[...].astype(F32)
        put_shares(total, grp[0], share_refs)
        own, other = loss_ref[...], other_loss_ref[...]
        here = jnp.zeros(own.shape, I32) + core[0]
        all_loss_ref[0:1, :] = jnp.where(here == 0, own, other)
        all_loss_ref[1:2, :] = jnp.where(here == 0, other, own)
        gw[...] = jnp.zeros_like(gw)
        grel[...] = jnp.zeros_like(grel)
        for s in range(planes):
            at = lax.rem(plane[0] - s + planes, planes)
            source = send_ref.at[plane[0]] if s == 0 else got[s - 1]
            pltpu.make_async_copy(source.at[skip : skip + used, :], box.at[at], sems.at[at]).start()

    pltpu.make_async_copy(send_ref.at[0, skip : skip + used, :], box.at[j], sems.at[j]).wait()
    quarter = used - INFO_ROWS
    tiles = node_rows // 128
    count = tiles * quarter
    cut = [slice(t * 128, (t + 1) * 128) for t in range(tiles)]
    line = jnp.concatenate([box[j, INFO_ROWS:, at] for at in cut], axis=0).astype(F32)
    info = box[j, 0:INFO_ROWS, :].astype(F32)
    target = jnp.broadcast_to(info[1:2, 0:count], (128, count)).T[:, 0:1]
    spread = [jnp.where(target == t, line, 0.0) for t in range(tiles)]
    hi, lo = split(dot(jnp.concatenate(spread, axis=1).astype(BF), agg_grad_ref[...]))
    relation = lax.broadcasted_iota(I32, (grel.shape[0], count), 0).astype(F32)
    chosen = jnp.where(relation == info[0:1, 0:count], 1.0, 0.0).astype(BF)
    grel[...] = grel[...] - (dot(chosen, hi) + dot(chosen, lo))
    flipped = pre_ref[...].astype(F32).T.astype(BF)
    gw[0] = gw[0] + dot(flipped, agg_ref[...])
    gw[1] = gw[1] + dot(flipped, node_ref[...])

    @pl.when(j == pl.num_programs(0) - 1)
    def _():
        out_ref[0:width, :] = gw[0].T.astype(BF)
        out_ref[width : 2 * width, :] = gw[1].T.astype(BF)
        out_ref[2 * width :, :] = grel[...].astype(BF)


def sums_of_half(
    places, pre, agg, nodes, agg_grad, mine, theirs, loss, other_loss, send, got, skip, rel_rows, flips
):
    width = pre.shape[1]
    small = (mine, theirs, loss, other_loss)
    planes, send_rows, node_rows = send.shape
    tall = pl.BlockSpec((node_rows, width), lambda i, *a: (i, 0))
    anywhere = pl.BlockSpec(memory_space=pl.ANY)
    outs = [
        ((2 * width + rel_rows, width), BF),
        ((2, loss.shape[1]), F32),
        *share_shapes(*mine.shape, flips),
    ]
    return pl.pallas_call(
        functools.partial(sums_kernel, skip, planes),
        grid_spec=pltpu.PrefetchScalarGridSpec(
            num_scalar_prefetch=3,
            grid=(planes,),
            in_specs=[tall] * 4 + [fixed(x.shape) for x in small] + [anywhere] * planes,
            out_specs=[fixed(x) for x, _ in outs],
            scratch_shapes=[
                pltpu.VMEM(mine.shape, F32),
                pltpu.VMEM((2, width, width), F32),
                pltpu.VMEM((rel_rows, width), F32),
                pltpu.VMEM((planes, send_rows - skip, node_rows), BF),
                pltpu.SemaphoreType.DMA((planes,)),
            ],
        ),
        out_shape=shaped(*outs),
        compiler_params=params(planes <= 4, 14),
        cost_estimate=cost(20),
        name="sums_of_half",
    )(*places, pre, agg, nodes, agg_grad, *small, send, *got)


def shift_planes(x, by, cand_count):
    return lax.ppermute(x, "cand", [(i, (i + 2 * by) % cand_count) for i in range(cand_count)])


def swap_core(x, cand_count):
    return lax.ppermute(x, "cand", [(i, i ^ 1) for i in range(cand_count)])


def swap_grp(x, flip, grp_count):
    return lax.ppermute(x, "grp", [(i, i ^ flip) for i in range(grp_count)])


def total_kernel(a_ref, b_ref, gwin_ref, gwself_ref, grel_ref):
    start = 0
    for ref in (gwin_ref, gwself_ref, grel_ref):
        at = slice(start, start + ref.shape[0])
        ref[...] = a_ref[at, :].astype(F32) + b_ref[at, :].astype(F32)
        start += ref.shape[0]


def total_sums(a, b, rel_count):
    width = a.shape[1]
    outs = [((n, width), F32) for n in (width, width, rel_count)]
    return pl.pallas_call(
        total_kernel,
        in_specs=[pl.BlockSpec(memory_space=pltpu.VMEM)] * 2,
        out_specs=[pl.BlockSpec(memory_space=pltpu.VMEM)] * 3,
        out_shape=shaped(*outs),
        compiler_params=params(True, 12),
        name="total_sums",
    )(a, b)


def gather_planes(x, cand_count):
    return [x] + [shift_planes(x, s, cand_count) for s in range(1, cand_count // 2)]


def gather_stacks(here, block, grp_count):
    one, two = swap_grp(here, 1, grp_count), swap_grp(here, 2, grp_count)
    cut = here.shape[0] // block // 2 * block
    return [
        here,
        one,
        two,
        swap_grp(one[:cut], 2, grp_count),
        swap_grp(two[cut:], 1, grp_count),
    ]


def gather_pieces(planes, first, cand_count, grp_count):
    pieces = []
    for s in range(first, cand_count // 2):
        found = [planes[s]]
        for flip in range(1, grp_count):
            low, high = flip & -flip, flip - (flip & -flip)
            if high == 0:
                found.append(swap_grp(planes[s], flip, grp_count))
            elif s % 2:
                found.append(swap_grp(found[low], high, grp_count))
            else:
                found.append(swap_grp(found[high], low, grp_count))
        pieces += found
    return pieces


def swap_shares(parts, grp_count):
    return [swap_grp(part, flip + 1, grp_count) for flip, part in enumerate(parts)]


def body(
    node_emb,
    rel_emb,
    w_in,
    w_self,
    rel_score,
    mirror_blocks,
    adj_values,
    adj_source,
    adj_target,
    adj_relation,
    live_blocks,
    query_head,
    query_rel,
    allowed,
    true_tail,
):
    cand_count = lax.axis_size("cand")
    grp_count = lax.axis_size("grp")
    grp_index = lax.axis_index("grp").astype(I32)
    cand_index = lax.axis_index("cand").astype(I32)
    nodes = node_emb[0]
    node_rows, width = nodes.shape
    block = adj_values.shape[-1]
    tiles = node_rows // block
    share_rows = node_rows // grp_count
    plane_count = cand_count // 2
    plane, core = cand_index // 2, cand_index % 2
    half = plane_count * node_rows
    want = mirror_blocks.reshape(-1)
    total_q = query_head.shape[0]
    half_q = total_q // 2
    rel_rows = -(-rel_emb.shape[0] // 128) * 128

    own_share = lax.dynamic_slice_in_dim(nodes, grp_index * share_rows, share_rows, 0)
    their_want = swap_core(want, cand_count)
    stack = jnp.concatenate(gather_planes(own_share, cand_count)[1:])
    cat, send = fold(
        adj_values[0, 0],
        adj_source[0, 0],
        adj_target[0, 0],
        adj_relation[0, 0],
        live_blocks[0],
        want,
        core[None],
        tiles,
        rel_rows,
    )
    stack, cat, send = lax.optimization_barrier((stack, cat, send))
    nodes_at = [nodes, *gather_stacks(stack, share_rows, grp_count)]

    def own_half(x):
        return lax.dynamic_slice_in_dim(x, core * half_q, half_q, 0)

    def order(ids):
        cand = ids // node_rows
        return ((cand % 2) ^ core) * half + (cand // 2) * node_rows + ids % node_rows

    rel_q = jnp.take(rel_score, own_half(query_rel), axis=0)
    allowed_at = order(own_half(allowed) * block) // block
    block_ids = jnp.arange(2 * half // block, dtype=I32)
    hit = jnp.any(allowed_at.T[:, None, :] == block_ids[None, :, None], axis=0)
    bias = jnp.where(hit, 0.0, NEG_FILL).astype(F32)
    meta = jnp.concatenate(
        [
            jnp.broadcast_to(order(own_half(true_tail))[None], (8, half_q)),
            jnp.broadcast_to(order(own_half(query_head))[None], (8, half_q)),
        ]
    )
    *nodes_at, rel_q, bias, meta = lax.optimization_barrier((*nodes_at, rel_q, bias, meta))
    mine, theirs = pick(
        plane[None], grp_index[None], core[None], want, their_want, nodes_at, block
    )
    theirs = swap_core(theirs, cand_count)
    own, *parts = forward(
        core[None], grp_index[None], mine, theirs, cat, rel_emb, block, grp_count
    )
    own_agg = join([own, *swap_shares(parts, grp_count)], BF)
    agg_planes = gather_planes(own_agg, cand_count)
    agg_pieces = gather_pieces(agg_planes, 0, cand_count, grp_count)

    agg_pieces, rel_q, bias, meta = lax.optimization_barrier((agg_pieces, rel_q, bias, meta))
    half_agg, half_nodes, half_h, half_d, h_own = activate(
        plane[None], grp_index[None], agg_pieces, nodes_at, w_in, w_self
    )

    other_h = swap_core(half_h, cand_count)

    def send_to_plane(x, by):
        part = lax.dynamic_index_in_dim(x, (plane + by) % plane_count, 0, keepdims=False)
        return shift_planes(part, by, cand_count)

    send_after = lax.optimization_barrier((send, half_h))[0]
    got = [send_to_plane(send_after, by) for by in range(1, plane_count)]
    gs, qg, qb, loss, *out_grad = score(half_h, other_h, rel_q, bias, meta, block, total_q)
    gs, *more = lax.optimization_barrier((gs, *out_grad, *got))
    out_grad, got = more[: len(out_grad)], more[len(out_grad) :]
    other_loss = swap_core(loss, cand_count)
    out_grad = out_grad[0] if out_grad else rows(half, gs, qb, qg, meta, other_h, "rows_other")
    in_grad = swap_core(out_grad, cand_count)
    own_grad = rows(0, gs, qb, qg, meta, half_h, "rows_own")
    pre, agg_grad, mine, theirs, self_grad = backward(
        plane[None],
        grp_index[None],
        own_grad,
        in_grad,
        half_d,
        w_in,
        w_self,
        send,
        got,
        tiles,
        block,
    )
    sums, loss, own, *parts = sums_of_half(
        (plane[None], grp_index[None], core[None]),
        pre,
        half_agg,
        half_nodes,
        agg_grad,
        mine,
        swap_core(theirs, cand_count),
        loss,
        other_loss,
        send,
        got,
        2 * block,
        rel_rows,
        grp_count,
    )
    gwin, gwself, grel = total_sums(sums, swap_core(sums, cand_count), rel_emb.shape[0])
    own, gwin, gwself, grel = lax.optimization_barrier((own, gwin, gwself, grel))
    node_grad = join([own, self_grad, *swap_shares(parts, grp_count)], F32)
    return (
        h_own[None],
        loss.reshape(total_q),
        node_grad[None],
        grel,
        gwin,
        gwself,
    )


def solution(mesh):
    return jax.shard_map(
        body,
        mesh=mesh,
        in_specs=(
            P("cand", None, None),
            P("grp", None),
            P(),
            P(),
            P(),
            P("grp", "cand", None, None),
            P("grp", "cand", None, None, None),
            P("grp", "cand", None),
            P("grp", "cand", None),
            P("grp", "cand", None),
            P("grp", "cand"),
            P(),
            P(),
            P(),
            P(),
        ),
        out_specs=(P("cand", "grp", None), P(), P("cand", "grp", None), P("grp", None), P(), P()),
        check_vma=False,
    )
```
